256 devices in a mesh: ctx: 64 (over y, z, core), tp: 4 (over x).
Axes of the slice: x: 4, y: 4, z: 8, core: 2. Of those that a mesh axis runs over, the one named last changes fastest.
Arguments:
- frames: bfloat16 [16384, 2, 1024], P(('ctx', 'tp')), may hold values from -6 to 6
- lengths: int32 [2], replicated, may hold values from 8192 to 16384
- value_weight: bfloat16 [2, 1024, 1024], P(None, None, 'tp'), may hold values from -0.1875 to 0.1875
- gate_weight: bfloat16 [2, 1024, 1024], P(None, None, 'tp'), may hold values from -0.1875 to 0.1875
- tap_weights: float32 [2, 31, 1024], P(None, None, 'tp'), may hold values from -1 to 1
- norm_gain: float32 [2, 1024], P(None, 'tp'), may hold values from 0.5 to 2
- norm_shift: float32 [2, 1024], P(None, 'tp'), may hold values from -3 to 3
- project_weight: bfloat16 [2, 1024, 1024], P(None, 'tp'), may hold values from -0.1875 to 0.1875
- output_grad: bfloat16 [16384, 2, 1024], P(('ctx', 'tp')), may hold values from -6 to 6
Outputs:
- input_grad: float32 [16384, 2, 1024], P(('ctx', 'tp'))
- value_grad: float32 [2, 1024, 1024], P(None, 'ctx', 'tp')
- gate_grad: float32 [2, 1024, 1024], P(None, 'ctx', 'tp')
- project_grad: float32 [2, 1024, 1024], P(None, 'tp', 'ctx')
- tap_grad: float32 [2, 31, 1024], P(None, None, 'tp')
The draws below stay inside these ranges and needn't reach their ends.
All inputs are finite; a program needn't handle non-finite values.
Results may differ from the reference program's by a relative error of at most 0.025.
Values may be sent and summed in bfloat16 or wider, within the bound.
A program may use at most 128 MiB of HBM per device.

```python
import math
import jax
import jax.numpy as jnp
from jax import lax

D = 1024
KERNEL = 31
LAYERS = 2
FRAMES_DEV = 256
RECS = 2
FRAMES = 16384


def draw_frames(key, part):
    key = jax.random.fold_in(key, 11)
    noise_key, offset_key = jax.random.split(key, 2)
    blocks = FRAMES // FRAMES_DEV
    noise = jax.random.truncated_normal(noise_key, -4.0, 4.0, (blocks, FRAMES_DEV, RECS, D), jnp.float32)
    offsets = 2.0 * jax.random.truncated_normal(offset_key, -1.5, 1.5, (blocks, 1, 1, D), jnp.float32)
    values = jnp.clip(noise + offsets, -6.0, 6.0)
    return values.reshape(FRAMES, RECS, D).astype(jnp.bfloat16)


def level_of(rng, dims, pieces, least, largest):
    loudness = 1.0
    for dim, shards_of in pieces:
        heights = jax.random.uniform(jax.random.fold_in(jax.random.fold_in(rng, 6), dim), (shards_of,), jnp.float32, least / len(pieces), largest / len(pieces))
        loudness = loudness * jnp.repeat(jnp.exp(heights), dims[dim] // shards_of).reshape((-1,) + (1,) * (len(dims) - 1 - dim))
    return loudness


def normal_values(stream_key, extent, scale, bound, shards=(), kind=jnp.bfloat16):
    loudness = level_of(stream_key, extent, shards, -0.22, 0.18) if shards else 1.0
    array = jax.random.normal(stream_key, extent, jnp.float32) * scale * loudness
    return jnp.minimum(jnp.maximum(array, -bound), bound).astype(kind)


def setup_inputs(seed: int = 0) -> dict:
    key_list = jax.random.split(jax.random.key(seed), 10)
    frames = draw_frames(jax.random.fold_in(key_list[9], 71), 0)
    lengths = jax.random.randint(key_list[1], (RECS,), FRAMES // 2, FRAMES + 1).astype(jnp.int32)
    value_weight = normal_values(key_list[2], (LAYERS, D, D), D ** -0.5, 0.1875, ((2, 4),))
    gate_weight = normal_values(key_list[3], (LAYERS, D, D), D ** -0.5, 0.1875, ((2, 4),))
    tap_weights = normal_values(key_list[4], (LAYERS, KERNEL, D), KERNEL ** -0.5, 1.0, ((2, 4),), jnp.float32)
    norm_gain = jnp.clip(jnp.exp(math.log(2.0) - 1.3862944 * jax.random.uniform(key_list[5], (LAYERS, D), jnp.float32) ** level_of(key_list[5], (LAYERS, D), ((1, 4),), -0.2, 0.2)), 0.5, 2.0)
    norm_shift = normal_values(key_list[6], (LAYERS, D), 0.5, 3.0, ((1, 4),), jnp.float32)
    project_weight = normal_values(key_list[7], (LAYERS, D, D), D ** -0.5, 0.1875, ((1, 4),))
    output_grad = normal_values(key_list[8], (FRAMES, RECS, D), 1.0, 6.0, ((0, 256),))
    return dict(frames=frames, lengths=lengths, value_weight=value_weight, gate_weight=gate_weight, tap_weights=tap_weights, norm_gain=norm_gain, norm_shift=norm_shift, project_weight=project_weight, output_grad=output_grad)


EPSILON = 1e-05

def depthwise(signal, taps, reach):
    length = signal.shape[0]
    padded = jnp.pad(signal, ((reach, reach), (0, 0), (0, 0)))
    result = taps[0] * padded[0:length]
    for offset in range(1, 2 * reach + 1):
        result = result + taps[offset] * padded[offset:offset + length]
    return (result, padded)

def depthwise_back(grads, taps, reach):
    length = grads.shape[0]
    padded = jnp.pad(grads, ((reach, reach), (0, 0), (0, 0)))
    result = taps[0] * padded[2 * reach:2 * reach + length]
    for offset in range(1, 2 * reach + 1):
        result = result + taps[offset] * padded[2 * reach - offset:2 * reach - offset + length]
    return result

def reference(frames, lengths, value_weight, gate_weight, tap_weights, norm_gain, norm_shift, project_weight, output_grad):
    length, record_count, width = frames.shape
    reach = tap_weights.shape[1] // 2
    positions = jnp.arange(length, dtype=jnp.int32)[:, None]
    valid = (positions < lengths[None, :]).astype(jnp.float32)[:, :, None]
    total = jnp.sum(lengths).astype(jnp.float32)
    saved = []
    hidden = frames
    for layer in range(LAYERS):
        rows32 = hidden.astype(jnp.float32)
        centered = rows32 - lax.optimization_barrier(jnp.mean(rows32, axis=-1, keepdims=True))
        ln_scale = jax.lax.rsqrt(lax.optimization_barrier(jnp.mean(centered * centered, axis=-1, keepdims=True)) + EPSILON)
        normed = centered * ln_scale
        normed_low = normed.astype(jnp.bfloat16)
        flat_low = normed_low.reshape(-1, width)
        value_pre = jnp.dot(flat_low, value_weight[layer], preferred_element_type=jnp.float32).reshape(length, record_count, width)
        gate_pre = jnp.dot(flat_low, gate_weight[layer], preferred_element_type=jnp.float32).reshape(length, record_count, width)
        glu = (value_pre * jax.nn.sigmoid(gate_pre) * valid).astype(jnp.bfloat16)
        mixed, widened = depthwise(glu.astype(jnp.float32), tap_weights[layer], reach)
        chan_mean = lax.optimization_barrier(jnp.sum(mixed * valid, axis=(0, 1))) / total
        chan_var = lax.optimization_barrier(jnp.sum(((mixed - chan_mean) * valid) ** 2, axis=(0, 1))) / total
        chan_scale = jax.lax.rsqrt(chan_var + EPSILON)
        scaled = (mixed - chan_mean) * chan_scale
        shifted = norm_gain[layer] * scaled + norm_shift[layer]
        activated = (jax.nn.silu(shifted) * valid).astype(jnp.bfloat16)
        saved.append((normed, ln_scale, flat_low, value_pre, gate_pre, widened, scaled, shifted, chan_scale, activated))
        if layer + 1 < LAYERS:
            branch = jnp.dot(activated.reshape(-1, width), project_weight[layer], preferred_element_type=jnp.float32)
            hidden = (rows32 + branch.reshape(length, record_count, width)).astype(jnp.bfloat16)
    upstream = output_grad.astype(jnp.float32)
    value_list, gate_list, project_list, tap_list = ([], [], [], [])
    for layer in range(LAYERS - 1, -1, -1):
        normed, ln_scale, flat_low, value_pre, gate_pre, widened, scaled, shifted, chan_scale, activated = saved[layer]
        upstream_low = upstream.astype(jnp.bfloat16).reshape(-1, width)
        act_grad = jnp.dot(upstream_low, project_weight[layer].T, preferred_element_type=jnp.float32).reshape(length, record_count, width)
        project_list.append(jnp.dot(activated.reshape(-1, width).T, upstream_low, preferred_element_type=jnp.float32))
        sig_shift = jax.nn.sigmoid(shifted)
        shift_grad = act_grad * sig_shift * (1.0 + shifted * (1.0 - sig_shift)) * valid
        first = lax.optimization_barrier(jnp.sum(shift_grad, axis=(0, 1))) / total
        second = lax.optimization_barrier(jnp.sum(shift_grad * scaled, axis=(0, 1))) / total
        mixed_grad = norm_gain[layer] * chan_scale * (shift_grad - first - scaled * second) * valid
        tap_list.append(jnp.stack([lax.optimization_barrier(jnp.sum(widened[offset:offset + length] * mixed_grad, axis=(0, 1))) for offset in range(2 * reach + 1)]))
        glu_grad = depthwise_back(mixed_grad, tap_weights[layer], reach) * valid
        sig_gate = jax.nn.sigmoid(gate_pre)
        value_low = (glu_grad * sig_gate).astype(jnp.bfloat16).reshape(-1, width)
        gate_low = (glu_grad * value_pre * sig_gate * (1.0 - sig_gate)).astype(jnp.bfloat16).reshape(-1, width)
        value_list.append(jnp.dot(flat_low.T, value_low, preferred_element_type=jnp.float32))
        gate_list.append(jnp.dot(flat_low.T, gate_low, preferred_element_type=jnp.float32))
        normed_grad = jnp.dot(value_low, value_weight[layer].T, preferred_element_type=jnp.float32) + jnp.dot(gate_low, gate_weight[layer].T, preferred_element_type=jnp.float32)
        normed_grad = normed_grad.reshape(length, record_count, width)
        row_grad = ln_scale * (normed_grad - lax.optimization_barrier(jnp.mean(normed_grad, axis=-1, keepdims=True)) - normed * lax.optimization_barrier(jnp.mean(normed_grad * normed, axis=-1, keepdims=True)))
        upstream = upstream + row_grad
    return (upstream, jnp.stack(value_list[::-1]), jnp.stack(gate_list[::-1]), jnp.stack(project_list[::-1]), jnp.stack(tap_list[::-1]))
```

```python
import functools

import jax
import jax.numpy as jnp
from jax import lax
from jax.experimental import pallas as pl
from jax.experimental.pallas import tpu as pltpu
from jax.sharding import PartitionSpec as P

EPSILON = 1e-05
MESH = pl.DeviceIdType.MESH


def grid_of(ctx):
    return {64: (4, 8, 2), 8: (2, 2, 2), 4: (2, 1, 2)}[ctx]


def place(ctx):
    ny, nz, nc = grid_of(ctx)
    me = lax.axis_index("ctx")
    return me // (nz * nc), (me // nc) % nz, me % nc


def greet(peers):
    barrier = pltpu.get_barrier_semaphore()
    for peer in peers:
        pl.semaphore_signal(barrier, inc=1, device_id={"ctx": peer}, device_id_type=MESH)
    pl.semaphore_wait(barrier, len(peers))


def exchange(buf, me, count, target, send_sem, recv_sem):
    copies = []
    for step in range(1, count):
        peer = lax.rem(me + step, count)
        copy = pltpu.make_async_remote_copy(
            src_ref=buf.at[me],
            dst_ref=buf.at[me],
            send_sem=send_sem.at[step],
            recv_sem=recv_sem.at[me],
            device_id={"ctx": target(peer)},
            device_id_type=MESH,
        )
        copy.start()
        copies.append(copy)
    for step in range(1, count):
        peer = lax.rem(me + step, count)
        pltpu.make_async_remote_copy(
            src_ref=buf.at[peer],
            dst_ref=buf.at[peer],
            send_sem=send_sem.at[step],
            recv_sem=recv_sem.at[peer],
            device_id={"ctx": target(peer)},
            device_id_type=MESH,
        ).wait_recv()
    for copy in copies:
        copy.wait_send()


def merge_moments(buf, count):
    parts = [buf[i] for i in range(count)]
    num = parts[0][2:3]
    tot = parts[0][0:1]
    for p in parts[1:]:
        num = num + p[2:3]
        tot = tot + p[0:1]
    mean = tot / jnp.maximum(num, 1.0)
    square = jnp.zeros_like(mean)
    for p in parts:
        gap = p[0:1] / jnp.maximum(p[2:3], 1.0) - mean
        square = square + (p[1:2] + p[2:3] * gap * gap)
    return jnp.concatenate([tot, square, num, jnp.zeros_like(parts[0][3:])], axis=0)


def merge_sum(buf, count):
    total = buf[0]
    for i in range(1, count):
        total = total + buf[i]
    return total


def reduce_kernel(ctx, merge, x_ref, o_ref, first, second, send1, recv1, send2, recv2):
    ny, nz, nc = grid_of(ctx)
    y, z, c = place(ctx)
    one = lambda p: ((p // nc) * nz + z) * nc + p % nc
    two = lambda p: (y * nz + p) * nc + c
    mine = y * nc + c
    greet(
        [one(lax.rem(mine + s, ny * nc)) for s in range(1, ny * nc)]
        + [two(lax.rem(z + s, nz)) for s in range(1, nz)]
    )
    first[mine] = x_ref[...]
    exchange(first, mine, ny * nc, one, send1, recv1)
    second[z] = merge(first, ny * nc)
    exchange(second, z, nz, two, send2, recv2)
    o_ref[...] = merge(second, nz)


def all_reduce(x, merge, cid):
    ctx = lax.axis_size("ctx")
    ny, nz, nc = grid_of(ctx)
    return pl.pallas_call(
        functools.partial(reduce_kernel, ctx, merge),
        out_shape=jax.ShapeDtypeStruct(x.shape, x.dtype),
        in_specs=[pl.BlockSpec(memory_space=pltpu.VMEM)],
        out_specs=pl.BlockSpec(memory_space=pltpu.VMEM),
        scratch_shapes=[
            pltpu.VMEM((ny * nc,) + x.shape, x.dtype),
            pltpu.VMEM((nz,) + x.shape, x.dtype),
            pltpu.SemaphoreType.DMA((ny * nc,)),
            pltpu.SemaphoreType.DMA((ny * nc,)),
            pltpu.SemaphoreType.DMA((nz,)),
            pltpu.SemaphoreType.DMA((nz,)),
        ],
        compiler_params=pltpu.CompilerParams(collective_id=cid, has_side_effects=True),
    )(x)


def scatter_kernel(ctx, x_ref, o_ref, in1, in2, in3, out2, out3, ssem, rsem):
    ny, nz, nc = grid_of(ctx)
    y, z, c = place(ctx)
    k = x_ref.shape[0]
    ids_c = [((y * nz + z) * nc + lax.rem(c + s, nc)) for s in range(1, nc)]
    ids_y = [((lax.rem(y + s, ny) * nz + z) * nc + c) for s in range(1, ny)]
    ids_z = [((y * nz + lax.rem(z + s, nz)) * nc + c) for s in range(1, nz)]
    greet(ids_c + ids_y + ids_z)

    def send(src, dst, sem, target):
        copy = pltpu.make_async_remote_copy(
            src_ref=src,
            dst_ref=dst,
            send_sem=ssem.at[sem],
            recv_sem=rsem.at[sem],
            device_id={"ctx": target},
            device_id_type=MESH,
        )
        copy.start()
        return copy

    other = lax.rem(c + 1, nc)
    copy = send(x_ref.at[:, :, :, other], in1, 0, ids_c[0])
    copy.wait()

    def add1(i, carry):
        a, b = i // (ny * nz), i % (ny * nz)
        iy, iz = b // nz, b % nz
        out2[a, iy, iz] = (
            x_ref[a, iy, iz, c].astype(jnp.float32) + in1[a, iy, iz].astype(jnp.float32)
        ).astype(jnp.bfloat16)
        return carry

    lax.fori_loop(0, k * ny * nz, add1, 0)
    copies = []
    for s in range(1, ny):
        copies.append(send(out2.at[:, lax.rem(y + s, ny)], in2.at[s - 1], s, ids_y[s - 1]))
    for copy in copies:
        copy.wait()

    def add2(i, carry):
        a, iz = i // nz, i % nz
        total = out2[a, y, iz].astype(jnp.float32)
        for s in range(ny - 1):
            total = total + in2[s, a, iz].astype(jnp.float32)
        out3[a, iz] = total.astype(jnp.bfloat16)
        return carry

    lax.fori_loop(0, k * nz, add2, 0)
    copies = []
    for s in range(1, nz):
        copies.append(send(out3.at[:, lax.rem(z + s, nz)], in3.at[s - 1], ny + s, ids_z[s - 1]))
    for copy in copies:
        copy.wait()

    def add3(a, carry):
        total = out3[a, z].astype(jnp.float32)
        for s in range(nz - 1):
            total = total + in3[s, a].astype(jnp.float32)
        o_ref[a] = total
        return carry

    lax.fori_loop(0, k, add3, 0)


def scatter_rows(x, cid):
    ctx = lax.axis_size("ctx")
    ny, nz, nc = grid_of(ctx)
    k, rows, width = x.shape
    piece = rows // ctx
    x = x.reshape(k, ny, nz, nc, piece, width)
    return pl.pallas_call(
        functools.partial(scatter_kernel, ctx),
        out_shape=jax.ShapeDtypeStruct((k, piece, width), jnp.float32),
        in_specs=[pl.BlockSpec(memory_space=pltpu.VMEM)],
        out_specs=pl.BlockSpec(memory_space=pltpu.VMEM),
        scratch_shapes=[
            pltpu.VMEM((k, ny, nz, piece, width), x.dtype),
            pltpu.VMEM((ny - 1, k, nz, piece, width), x.dtype),
            pltpu.VMEM((max(nz - 1, 1), k, piece, width), x.dtype),
            pltpu.VMEM((k, ny, nz, piece, width), x.dtype),
            pltpu.VMEM((k, nz, piece, width), x.dtype),
            pltpu.SemaphoreType.DMA((ny + nz,)),
            pltpu.SemaphoreType.DMA((ny + nz,)),
        ],
        compiler_params=pltpu.CompilerParams(
            collective_id=cid, has_side_effects=True, vmem_limit_bytes=40 * 1024 * 1024
        ),
    )(x)


def padded(block, sides, width):
    for axis, dim in sides:
        count = lax.axis_size(axis)
        forward = [(i, i + 1) for i in range(count - 1)]
        backward = [(target, source) for source, target in forward]
        low = lax.ppermute(
            lax.slice_in_dim(block, block.shape[dim] - width, None, axis=dim), axis, forward
        )
        high = lax.ppermute(lax.slice_in_dim(block, 0, width, axis=dim), axis, backward)
        block = jnp.concatenate([low, block, high], axis=dim)
    return block


def on_device(
    frames,
    lengths,
    value_weight,
    gate_weight,
    tap_weights,
    norm_gain,
    norm_shift,
    project_weight,
    output_grad,
):
    local_rows = frames.shape[0]
    frame_count = local_rows * lax.axis_size("tp")
    reach = tap_weights.shape[1] // 2
    layer_count = value_weight.shape[0]
    width = tap_weights.shape[2]
    first_frame = lax.axis_index("ctx") * frame_count
    positions = first_frame + jnp.arange(frame_count, dtype=jnp.int32)[:, None]
    valid = (positions < lengths[None, :]).astype(jnp.float32)[:, :, None]
    total = jnp.sum(lengths).astype(jnp.float32)
    local_count = jnp.sum(jnp.clip(lengths - first_frame, 0, frame_count)).astype(jnp.float32)
    stored_list = []
    hidden = frames
    for layer in range(layer_count):
        rows32 = hidden.astype(jnp.float32)
        centered = rows32 - jnp.mean(rows32, axis=-1, keepdims=True)
        ln_scale = lax.rsqrt(jnp.mean(centered * centered, axis=-1, keepdims=True) + EPSILON)
        normed = centered * ln_scale
        normed_low = normed.astype(jnp.bfloat16)
        gathered = lax.all_gather(normed_low, "tp", axis=0, tiled=True)
        value_pre = jnp.einsum(
            "tbd,dc->tbc", gathered, value_weight[layer], preferred_element_type=jnp.float32
        )
        gate_pre = jnp.einsum(
            "tbd,dc->tbc", gathered, gate_weight[layer], preferred_element_type=jnp.float32
        )
        glu = (value_pre * jax.nn.sigmoid(gate_pre) * valid).astype(jnp.bfloat16)
        widened = padded(glu, (("ctx", 0),), reach).astype(jnp.float32)
        taps = tap_weights[layer]
        mixed = taps[0] * widened[0:frame_count]
        for offset in range(1, 2 * reach + 1):
            mixed = mixed + taps[offset] * widened[offset : offset + frame_count]
        local_sum = jnp.sum(mixed * valid, axis=(0, 1))
        local_mean = local_sum / jnp.maximum(local_count, 1.0)
        local_square = jnp.sum(((mixed - local_mean) * valid) ** 2, axis=(0, 1))
        moments = jnp.concatenate(
            [
                local_sum[None],
                local_square[None],
                jnp.full((1, width), local_count),
                jnp.zeros((5, width), jnp.float32),
            ]
        )
        moments = all_reduce(moments, merge_moments, 0)
        chan_mean = moments[0] / total
        chan_var = moments[1] / total
        chan_scale = lax.rsqrt(chan_var + EPSILON)
        scaled = (mixed - chan_mean) * chan_scale
        shifted = norm_gain[layer] * scaled + norm_shift[layer]
        activated = (jax.nn.silu(shifted) * valid).astype(jnp.bfloat16)
        stored_list.append(
            (
                normed,
                ln_scale,
                gathered,
                value_pre,
                gate_pre,
                widened,
                scaled,
                shifted,
                chan_scale,
                activated,
            )
        )
        if layer + 1 < layer_count:
            branch = lax.psum_scatter(
                jnp.einsum(
                    "tbc,cd->tbd",
                    activated,
                    project_weight[layer],
                    preferred_element_type=jnp.float32,
                ).astype(jnp.bfloat16),
                "tp",
                scatter_dimension=0,
                tiled=True,
            ).astype(jnp.float32)
            hidden = (rows32 + branch).astype(jnp.bfloat16)
    upstream = output_grad.astype(jnp.float32)
    weight_terms = [None] * (3 * layer_count)
    tap_list = [None] * layer_count
    for layer in range(layer_count - 1, -1, -1):
        (
            normed,
            ln_scale,
            gathered,
            value_pre,
            gate_pre,
            widened,
            scaled,
            shifted,
            chan_scale,
            activated,
        ) = stored_list[layer]
        upstream_all = lax.all_gather(upstream.astype(jnp.bfloat16), "tp", axis=0, tiled=True)
        act_grad = jnp.einsum(
            "tbd,cd->tbc", upstream_all, project_weight[layer], preferred_element_type=jnp.float32
        )
        weight_terms[3 * layer + 2] = jnp.einsum(
            "tbd,tbc->dc", upstream_all, activated, preferred_element_type=jnp.float32
        ).astype(jnp.bfloat16)
        sig_shift = jax.nn.sigmoid(shifted)
        shift_grad = act_grad * sig_shift * (1.0 + shifted * (1.0 - sig_shift)) * valid
        sums = jnp.concatenate(
            [
                jnp.sum(shift_grad, axis=(0, 1))[None],
                jnp.sum(shift_grad * scaled, axis=(0, 1))[None],
                jnp.zeros((6, width), jnp.float32),
            ]
        )
        sums = all_reduce(sums, merge_sum, 1)
        mixed_grad = (
            norm_gain[layer]
            * chan_scale
            * (shift_grad - sums[0] / total - scaled * (sums[1] / total))
            * valid
        )
        wide_grad = padded(mixed_grad.astype(jnp.bfloat16), (("ctx", 0),), reach).astype(
            mixed_grad.dtype
        )
        tap_list[layer] = jnp.stack(
            [
                jnp.sum(widened[offset : offset + frame_count] * mixed_grad, axis=(0, 1))
                for offset in range(2 * reach + 1)
            ]
            + [jnp.zeros((width,), jnp.float32)]
        )
        taps = tap_weights[layer]
        glu_grad = taps[0] * wide_grad[2 * reach : 2 * reach + frame_count]
        for offset in range(1, 2 * reach + 1):
            glu_grad = (
                glu_grad
                + taps[offset] * wide_grad[2 * reach - offset : 2 * reach - offset + frame_count]
            )
        glu_grad = glu_grad * valid
        sig_gate = jax.nn.sigmoid(gate_pre)
        value_low = (glu_grad * sig_gate).astype(jnp.bfloat16)
        gate_low = (glu_grad * value_pre * sig_gate * (1.0 - sig_gate)).astype(jnp.bfloat16)
        weight_terms[3 * layer] = jnp.einsum(
            "tbd,tbc->dc", gathered, value_low, preferred_element_type=jnp.float32
        ).astype(jnp.bfloat16)
        weight_terms[3 * layer + 1] = jnp.einsum(
            "tbd,tbc->dc", gathered, gate_low, preferred_element_type=jnp.float32
        ).astype(jnp.bfloat16)
        normed_grad = lax.psum_scatter(
            (
                jnp.einsum(
                    "tbc,dc->tbd",
                    value_low,
                    value_weight[layer],
                    preferred_element_type=jnp.float32,
                )
                + jnp.einsum(
                    "tbc,dc->tbd", gate_low, gate_weight[layer], preferred_element_type=jnp.float32
                )
            ).astype(jnp.bfloat16),
            "tp",
            scatter_dimension=0,
            tiled=True,
        ).astype(jnp.float32)
        row_grad = ln_scale * (
            normed_grad
            - jnp.mean(normed_grad, axis=-1, keepdims=True)
            - normed * jnp.mean(normed_grad * normed, axis=-1, keepdims=True)
        )
        upstream = upstream + row_grad
    parts = scatter_rows(jnp.stack(weight_terms), 2)
    parts = parts.reshape((layer_count, 3) + parts.shape[1:])
    tap_all = all_reduce(jnp.concatenate(tap_list), merge_sum, 3)
    tap_all = tap_all.reshape(layer_count, -1, width)[:, : 2 * reach + 1]
    return (
        upstream,
        parts[:, 0],
        parts[:, 1],
        jnp.swapaxes(parts[:, 2], 1, 2),
        tap_all,
    )


def solution(mesh):
    in_specs = (
        P(("ctx", "tp"), None, None),
        P(),
        P(None, None, "tp"),
        P(None, None, "tp"),
        P(None, None, "tp"),
        P(None, "tp"),
        P(None, "tp"),
        P(None, "tp", None),
        P(("ctx", "tp"), None, None),
    )
    out_specs = (
        P(("ctx", "tp"), None, None),
        P(None, "ctx", "tp"),
        P(None, "ctx", "tp"),
        P(None, "tp", "ctx"),
        P(None, None, "tp"),
    )
    return jax.shard_map(
        on_device, mesh=mesh, in_specs=in_specs, out_specs=out_specs, check_vma=False
    )
```

```python
import functools

import jax
import jax.numpy as jnp
from jax import lax
from jax.experimental import pallas as pl
from jax.experimental.pallas import tpu as pltpu
from jax.sharding import PartitionSpec as P

EPSILON = 1e-05
MESH = pl.DeviceIdType.MESH
F32, BF16 = jnp.float32, jnp.bfloat16
TAPS, REACH = 31, 15
LANES = 128
STREAMS, SEG = 4, 16
ROWS = SEG * 8
MAIN = REACH * 8
WIDE = (SEG + 2 * REACH) * 8


def grid_of(ctx):
    return {64: (4, 8, 2), 8: (2, 2, 2)}[ctx]


def rows_of(slot, first=0, count=ROWS):
    return pl.ds(pl.multiple_of(slot * ROWS + first, 16), count)


def sigmoid(v):
    return 1.0 / (1.0 + jnp.exp(-v))


def fused(
    ctx,
    tp,
    frames,
    og,
    lengths,
    vw,
    gw,
    pw,
    taps,
    gain,
    shift,
    up,
    value_out,
    gate_out,
    project_out,
    tap_out,
    val,
    gath,
    ups,
    part,
    land,
    normed,
    lnscale,
    fv,
    fg,
    scaled,
    ds,
    act,
    glu,
    wide,
    lows,
    halo,
    first,
    second,
    tapsum,
    tap1,
    tap2,
    wt,
    in1,
    out2,
    in2,
    out3,
    in3,
    ssem,
    rsem,
):
    ny, nz, nc = grid_of(ctx)
    pos = lax.axis_index("ctx")
    x = lax.axis_index("tp")
    y, z, c = pos // (nz * nc), (pos // nc) % nz, pos % nc
    depth = gath.shape[2]
    columns = value_out.shape[2]

    def to_x(p):
        return {"tp": p}

    def to_yc(p):
        return {"ctx": ((p // nc) * nz + z) * nc + p % nc}

    def to_y(p):
        return {"ctx": (p * nz + z) * nc + c}

    def to_z(p):
        return {"ctx": (y * nz + p) * nc + c}

    def to_c(p):
        return {"ctx": (y * nz + z) * nc + p}

    yc = y * nc + c
    following = {"ctx": lax.rem(pos + 1, ctx)}
    previous = {"ctx": lax.rem(pos + ctx - 1, ctx)}

    barrier = pltpu.get_barrier_semaphore()
    peers = [to_x(lax.rem(x + s, tp)) for s in range(1, tp)]
    peers += [to_yc(lax.rem(yc + s, ny * nc)) for s in range(1, ny * nc)]
    peers += [to_z(lax.rem(z + s, nz)) for s in range(1, nz)]
    peers += [following, previous]
    for peer in peers:
        pl.semaphore_signal(barrier, inc=1, device_id=peer, device_id_type=MESH)
    pl.semaphore_wait(barrier, len(peers))

    taken = [0]

    def take(n):
        taken[0] += n
        return taken[0] - n

    def remote(src, dst, send, recv, target):
        return pltpu.make_async_remote_copy(
            src_ref=src,
            dst_ref=dst,
            send_sem=ssem.at[send],
            recv_sem=rsem.at[recv],
            device_id=target,
            device_id_type=MESH,
        )

    class Exchange:
        def __init__(self, count, me, target, src, dst, order=None):
            self.count, self.me, self.target, self.src, self.dst = count, me, target, src, dst
            self.base = take(count)
            self.order = order or list(range(1, count))

        def peer(self, step):
            return lax.rem(self.me + step, self.count)

        def send(self, step):
            p = self.peer(step)
            remote(
                self.src(p), self.dst(self.me), self.base + step, self.base + self.me, self.target(p)
            ).start()

        def start(self):
            for step in self.order:
                self.send(step)

        def landed(self, step):
            p = self.peer(step)
            remote(
                self.src(p), self.dst(p), self.base + step, self.base + p, self.target(p)
            ).wait_recv()

        def sent(self):
            for step in self.order:
                p = self.peer(step)
                remote(
                    self.src(p), self.dst(self.me), self.base + step, self.base + self.me, self.target(p)
                ).wait_send()

        def finish(self):
            for step in self.order:
                self.landed(step)
            self.sent()

    far_last = [1, 3, 2] if tp == 4 else list(range(1, tp))
    far_first = [2, 1, 3] if tp == 4 else list(range(1, tp))

    len0, len1 = lengths[0], lengths[1]
    start_frame = pos * (tp * STREAMS * SEG)
    t_in = lax.broadcasted_iota(jnp.int32, (SEG, 8, LANES), 0)
    sub = lax.broadcasted_iota(jnp.int32, (SEG, 8, LANES), 1)
    limit = jnp.where(sub % 2 == 0, len0, len1)
    for s in range(tp):
        frame = start_frame + s * (STREAMS * SEG) + (sub // 2) * SEG + t_in
        val[s] = jnp.where(frame < limit, 1.0, 0.0).astype(F32).reshape(ROWS, LANES)
    span = tp * STREAMS * SEG
    total = (len0 + len1).astype(F32)
    local_count = (
        jnp.clip(len0 - start_frame, 0, span) + jnp.clip(len1 - start_frame, 0, span)
    ).astype(F32)

    def halves(h):
        return slice(h * LANES, (h + 1) * LANES)

    def reduce_tile(u, rows, merge, meanwhile=None):
        first[u, yc] = jnp.zeros((8, LANES), F32)
        for i, row in enumerate(rows):
            first[u, yc, i : i + 1, :] = row
        one = Exchange(
            ny * nc, yc, to_yc, lambda p: first.at[u, yc], lambda p: first.at[u, p]
        )
        one.start()
        if meanwhile is not None:
            meanwhile()
        one.finish()
        second[u, z] = merge([first[u, i] for i in range(ny * nc)])
        two = Exchange(nz, z, to_z, lambda p: second.at[u, z], lambda p: second.at[u, p])
        two.start()
        two.finish()
        return merge([second[u, i] for i in range(nz)])

    def merge_sum(tiles):
        whole = tiles[0]
        for tile in tiles[1:]:
            whole = whole + tile
        return whole

    def merge_moments(tiles):
        whole = merge_sum(tiles)
        mean = whole[0:2] / jnp.maximum(whole[4:5], 1.0)
        square = whole[2:4]
        for tile in tiles:
            gap = tile[0:2] / jnp.maximum(tile[4:5], 1.0) - mean
            square = square + tile[4:5] * gap * gap
        return jnp.concatenate([whole[0:2], square, whole[4:8]], axis=0)

    def fold(v):
        return jnp.sum(v.reshape(SEG, 8, LANES), axis=0)

    tile_sub = lax.broadcasted_iota(jnp.int32, (REACH, 8, LANES), 1)

    def widen(e, s):
        for h in range(2):
            cur = wide[e, h, s, MAIN + 8 : MAIN + ROWS].reshape(REACH, 8, LANES)
            old = wide[e, h, s - 1, MAIN + 8 : MAIN + ROWS].reshape(REACH, 8, LANES)
            low = jnp.where(tile_sub < 2, pltpu.roll(old, 2, 1), pltpu.roll(cur, 2, 1))
            wide[e, h, s, 0:MAIN] = low.reshape(MAIN, LANES)
            cur = wide[e, h, s, MAIN : MAIN + ROWS - 8].reshape(REACH, 8, LANES)
            new = wide[e, h, s + 1, MAIN : MAIN + ROWS - 8].reshape(REACH, 8, LANES)
            high = jnp.where(tile_sub >= 6, pltpu.roll(new, 6, 1), pltpu.roll(cur, 6, 1))
            wide[e, h, s, MAIN + ROWS : WIDE] = high.reshape(MAIN, LANES)

    def convolve(e, layer, h, s, forward):
        result = None
        for j in range(TAPS):
            at = (j if forward else TAPS - 1 - j) * 8
            term = taps[layer, j : j + 1, halves(h)] * wide[e, h, s, at : at + ROWS]
            result = term if result is None else result + term
        return result

    class Halo:
        def __init__(self, u):
            self.u = u
            base = take(2)
            self.up = remote(
                glu.at[rows_of(tp - 1)], halo.at[u, 0], base, base, following
            )
            self.down = remote(glu.at[rows_of(0)], halo.at[u, 1], base + 1, base + 1, previous)

        def start(self):
            self.up.start()
            self.down.start()

        def finish(self, e):
            self.up.wait()
            self.down.wait()
            has_low = (pos > 0).astype(F32)
            has_high = (pos < ctx - 1).astype(F32)
            for h in range(2):
                wide[e, h, 0, MAIN : MAIN + ROWS] = halo[self.u, 0, :, halves(h)].astype(F32) * has_low
                wide[e, h, tp + 1, MAIN : MAIN + ROWS] = (
                    halo[self.u, 1, :, halves(h)].astype(F32) * has_high
                )

    class Scatter:
        def __init__(self, layer):
            self.layer = layer
            other = lax.rem(c + 1, nc)
            base = take(1)
            self.core = remote(
                wt.at[layer, :, :, :, other], in1.at[layer], base, base, to_c(other)
            )
            self.ys = Exchange(
                ny, y, to_y, lambda p: out2.at[layer, :, p], lambda p: in2.at[layer, p]
            )
            self.zs = Exchange(
                nz, z, to_z, lambda p: out3.at[layer, :, p], lambda p: in3.at[layer, p]
            )

        def start(self):
            self.core.start()

        def after_core(self):
            layer = self.layer
            self.core.wait()

            def add(i, carry):
                a, b = i // ny, i % ny
                out2[layer, a, b] = (
                    wt[layer, a, b, :, c].astype(F32) + in1[layer, a, b].astype(F32)
                ).astype(BF16)
                return carry

            lax.fori_loop(0, 3 * ny, add, 0)
            self.ys.start()

        def after_y(self):
            layer = self.layer
            self.ys.finish()

            def add(a, carry):
                whole = out2[layer, a, y].astype(F32)
                for s in range(1, ny):
                    whole = whole + in2[layer, lax.rem(y + s, ny), a].astype(F32)
                out3[layer, a] = whole.astype(BF16)
                return carry

            lax.fori_loop(0, 3, add, 0)
            self.zs.start()

        def after_z(self):
            layer = self.layer
            self.zs.finish()
            for a, out in enumerate((value_out, gate_out, project_out)):
                whole = out3[layer, a, z].astype(F32)
                for s in range(1, nz):
                    whole = whole + in3[layer, lax.rem(z + s, nz), a].astype(F32)
                out[layer] = whole

    def weight_term(left, right, put):
        def step(i, carry):
            cols = pl.ds(pl.multiple_of(i * (depth // ny), depth // ny), depth // ny)
            whole = lax.dot_general(
                left[:, cols], right[...], (((0,), (0,)), ((), ())), preferred_element_type=F32
            )
            put(i, whole.astype(BF16))
            return carry

        lax.fori_loop(0, ny, step, 0)

    class TapSum:
        def __init__(self, layer):
            self.layer = layer
            self.one = Exchange(
                ny * nc, yc, to_yc, lambda p: tap1.at[layer, yc], lambda p: tap1.at[layer, p]
            )
            self.two = Exchange(
                nz, z, to_z, lambda p: tap2.at[layer, z], lambda p: tap2.at[layer, p]
            )

        def start(self):
            tap1[self.layer, yc] = tapsum[...].astype(BF16)
            self.one.start()

        def middle(self):
            self.one.finish()
            whole = tap1[self.layer, 0].astype(F32)
            for i in range(1, ny * nc):
                whole = whole + tap1[self.layer, i].astype(F32)
            tap2[self.layer, z] = whole.astype(BF16)
            self.two.start()

        def finish(self):
            self.two.finish()
            whole = tap2[self.layer, 0].astype(F32)
            for i in range(1, nz):
                whole = whole + tap2[self.layer, i].astype(F32)
            for h in range(2):
                tap_out[self.layer, :, halves(h)] = whole[h, 0:TAPS]

    CHUNK = 32

    def normalize(layer, rows_at):
        def step(i, carry):
            at = pl.ds(pl.multiple_of(i * CHUNK, CHUNK), CHUNK)
            rows = rows_at(i * CHUNK, at)
            centered = rows - jnp.mean(rows, axis=1, keepdims=True)
            scale = lax.rsqrt(jnp.mean(centered * centered, axis=1, keepdims=True) + EPSILON)
            out = centered * scale
            normed[layer, at] = out
            lnscale[layer, at] = jnp.broadcast_to(scale, (CHUNK, LANES))
            gath[layer, rows_of(x, i * CHUNK, CHUNK)] = out.astype(BF16)
            return carry

        lax.fori_loop(0, ROWS // CHUNK, step, 0)

    def landed_sum(u, first_row):
        whole = part[rows_of(x, first_row, CHUNK)].astype(F32)
        for s in range(1, tp):
            whole = whole + land[u, rows_of(lax.rem(x + s, tp), first_row, CHUNK)].astype(F32)
        return whole

    def gather_x(buf, which):
        return Exchange(
            tp,
            x,
            to_x,
            lambda p: buf.at[which, rows_of(x)],
            lambda p: buf.at[which, rows_of(p)],
            far_last,
        )

    def scatter_x(u):
        return Exchange(
            tp,
            x,
            to_x,
            lambda p: part.at[rows_of(p)],
            lambda p: land.at[u, rows_of(p)],
            far_first,
        )

    def back_rows(layer, u, put):
        def step(i, carry):
            at = pl.ds(pl.multiple_of(i * CHUNK, CHUNK), CHUNK)
            grad = landed_sum(u, i * CHUNK)
            unit = normed[layer, at]
            cross = jnp.mean(grad * unit, axis=1, keepdims=True)
            scale = lnscale[layer, at][:, 0:1]
            put(i, at, scale * (grad - jnp.mean(grad, axis=1, keepdims=True) - unit * cross))
            return carry

        lax.fori_loop(0, ROWS // CHUNK, step, 0)

    def forward(layer, after=None):
        gather = gather_x(gath, layer)
        gather.start()
        if after is not None:
            after()

        def block(s):
            rows = gath[layer, rows_of(s)]
            value = jnp.dot(rows, vw[layer], preferred_element_type=F32)
            gate = sigmoid(jnp.dot(rows, gw[layer], preferred_element_type=F32))
            for h in range(2):
                v, g = value[:, halves(h)], gate[:, halves(h)]
                keep = g * val[s]
                fv[layer, h, s] = keep
                fg[layer, h, s] = v * (1.0 - g) * keep
                low = (v * keep).astype(BF16)
                glu[rows_of(s), halves(h)] = low
                wide[layer, h, s + 1, MAIN : MAIN + ROWS] = low.astype(F32)

        def order(k):
            return lax.rem(x + k + (k == 2).astype(jnp.int32) - (k == 3).astype(jnp.int32), tp)

        block(x)
        for step in far_last:
            gather.landed(step)
            block(gather.peer(step))
        gather.sent()
        edge = Halo(layer)
        edge.start()

        def conv(s, carry):
            widen(layer, s + 1)
            sums = []
            for h in range(2):
                mixed = convolve(layer, layer, h, s + 1, True)
                scaled[layer, h, s] = mixed
                sums.append(carry[h] + fold(mixed * val[s]))
            return tuple(sums)

        zero = jnp.zeros((8, LANES), F32)
        sums = lax.fori_loop(1, tp - 1, conv, (zero, zero))
        edge.finish(layer)
        sums = lax.fori_loop(0, 2, lambda i, carry: conv(i * (tp - 1), carry), sums)
        sums = [jnp.sum(v, axis=0, keepdims=True) for v in sums]
        means = [v / jnp.maximum(local_count, 1.0) for v in sums]

        def spread(s, carry):
            out = []
            for h in range(2):
                gap = (scaled[layer, h, s] - means[h]) * val[s]
                out.append(carry[h] + fold(gap * gap))
            return tuple(out)

        squares = lax.fori_loop(0, tp, spread, (zero, zero))
        squares = [jnp.sum(v, axis=0, keepdims=True) for v in squares]
        count = jnp.zeros((1, LANES), F32) + local_count
        whole = reduce_tile(layer, sums + squares + [count], merge_moments)
        mean = [whole[h : h + 1] / total for h in range(2)]
        scale = [lax.rsqrt(whole[2 + h : 3 + h] / total + EPSILON) for h in range(2)]

        def activate(s):
            for h in range(2):
                unit = (scaled[layer, h, s] - mean[h]) * scale[h]
                shifted = gain[layer : layer + 1, halves(h)] * unit + shift[layer : layer + 1, halves(h)]
                sig = sigmoid(shifted)
                keep = sig * val[s]
                scaled[layer, h, s] = unit
                ds[layer, h, s] = keep * (1.0 + shifted * (1.0 - sig))
                act[layer, rows_of(s), halves(h)] = (shifted * keep).astype(BF16)

        return activate, scale

    def backward(layer, u, up_block, chan_scale, activate, between, after_send):
        zero = jnp.zeros((8, LANES), F32)

        def one_block(s, carry):
            if activate is not None:
                activate(s)
            grad = lax.dot_general(
                ups[layer, rows_of(s)], pw[layer], (((1,), (1,)), ((), ())), preferred_element_type=F32
            )
            sums = list(carry)
            for h in range(2):
                g = grad[:, halves(h)] * ds[layer, h, s]
                ds[layer, h, s] = g
                sums[h] = sums[h] + fold(g)
                sums[2 + h] = sums[2 + h] + fold(g * scaled[layer, h, s])
            return tuple(sums)

        sums = up_block(one_block, (zero,) * 4)
        sums = [jnp.sum(v, axis=0, keepdims=True) for v in sums]

        def project():
            def put(i, block):
                wt[layer, 2, i] = block.reshape(wt.shape[3:])

            weight_term(ups.at[layer], act.at[layer], put)

        whole = reduce_tile(2 + layer, sums, merge_sum, project)

        def mix(s, carry):
            for h in range(2):
                factor = gain[layer : layer + 1, halves(h)] * chan_scale[h]
                a, b = whole[h : h + 1] / total, whole[2 + h : 3 + h] / total
                grad = factor * (ds[layer, h, s] - a - scaled[layer, h, s] * b) * val[s]
                wide[2, h, s + 1, MAIN : MAIN + ROWS] = grad
                glu[rows_of(s), halves(h)] = grad.astype(BF16)
            return carry

        lax.fori_loop(0, tp, mix, 0)
        edge = Halo(2 + layer)
        edge.start()

        def tap(j, carry):
            at = pl.ds(pl.multiple_of(j * 8, 8), ROWS)
            for h in range(2):
                whole = None
                for s in range(1, tp + 1):
                    term = fold(wide[layer, h, s, at] * wide[2, h, s, MAIN : MAIN + ROWS])
                    whole = term if whole is None else whole + term
                tapsum[h, pl.ds(j, 1), :] = jnp.sum(whole, axis=0, keepdims=True)
            return carry

        lax.fori_loop(0, TAPS, tap, 0)
        tap_total = TapSum(layer)
        edge.finish(2)
        tap_total.start()
        between()

        send = scatter_x(u)

        def block(s):
            widen(2, s + 1)
            for h in range(2):
                grad = convolve(2, layer, h, s + 1, False)
                lows[rows_of(s), halves(h)] = (grad * fv[layer, h, s]).astype(BF16)
                lows[rows_of(s), slice(columns + h * LANES, columns + (h + 1) * LANES)] = (
                    grad * fg[layer, h, s]
                ).astype(BF16)
            whole = lax.dot_general(
                lows[rows_of(s), 0:columns],
                vw[layer],
                (((1,), (1,)), ((), ())),
                preferred_element_type=F32,
            ) + lax.dot_general(
                lows[rows_of(s), columns : 2 * columns],
                gw[layer],
                (((1,), (1,)), ((), ())),
                preferred_element_type=F32,
            )
            part[rows_of(s)] = whole.astype(BF16)

        for step in far_first:
            block(send.peer(step))
            send.send(step)
        block(x)

        def put(i, block):
            wt[layer, 0, i] = block[:, 0:columns].reshape(wt.shape[3:])
            wt[layer, 1, i] = block[:, columns:].reshape(wt.shape[3:])

        weight_term(gath.at[layer], lows, put)
        scatter = Scatter(layer)
        scatter.start()
        after_send(scatter, tap_total)
        send.finish()
        return scatter, tap_total

    tapsum[...] = jnp.zeros(tapsum.shape, F32)
    normalize(0, lambda first_row, at: frames[at].astype(F32))
    gather_up = gather_x(ups, 1)

    def send_up():
        ups[1, rows_of(x)] = og[...]
        gather_up.start()

    activate, scale0 = forward(0, send_up)
    branch = scatter_x(0)

    def project_block(s):
        activate(s)
        part[rows_of(s)] = jnp.dot(
            act[0, rows_of(s)], pw[0], preferred_element_type=F32
        ).astype(BF16)

    for step in far_first:
        project_block(branch.peer(step))
        branch.send(step)
    project_block(x)
    branch.finish()

    def hidden(first_row, at):
        return (frames[at].astype(F32) + landed_sum(0, first_row)).astype(BF16).astype(F32)

    normalize(1, hidden)
    activate, scale1 = forward(1)
    gather_up.finish()

    def all_blocks(block, carry):
        return lax.fori_loop(0, tp, block, carry)

    scatter1, taps1 = backward(
        1, 1, all_blocks, scale1, activate, lambda: None, lambda scatter, tap_total: tap_total.middle()
    )

    def next_up(i, at, grad):
        whole = og[at].astype(F32) + grad
        up[at] = whole
        ups[0, rows_of(x, i * CHUNK, CHUNK)] = whole.astype(BF16)

    back_rows(1, 1, next_up)
    gather0 = gather_x(ups, 0)
    gather0.start()
    scatter1.after_core()
    taps1.finish()

    def in_turn(block, carry):
        carry = block(x, carry)
        for step in far_last:
            gather0.landed(step)
            carry = block(gather0.peer(step), carry)
        gather0.sent()
        return carry

    def finish_first(scatter, tap_total):
        tap_total.middle()
        scatter.after_core()
        scatter1.after_z()

    scatter0, taps0 = backward(0, 2, in_turn, scale0, None, scatter1.after_y, finish_first)

    def last_up(i, at, grad):
        up[at] = up[at] + grad

    back_rows(0, 2, last_up)
    scatter0.after_y()
    taps0.finish()
    scatter0.after_z()


def scratch(ctx, tp, layers, depth, columns):
    ny, nz, nc = grid_of(ctx)
    rows = tp * ROWS
    piece = depth // ctx
    return [
        pltpu.VMEM((tp, ROWS, LANES), F32),
        pltpu.VMEM((layers, rows, depth), BF16),
        pltpu.VMEM((layers, rows, depth), BF16),
        pltpu.VMEM((rows, depth), BF16),
        pltpu.VMEM((3, rows, depth), BF16),
        pltpu.VMEM((layers, ROWS, depth), F32),
        pltpu.VMEM((layers, ROWS, LANES), F32),
        pltpu.VMEM((layers, 2, tp, ROWS, LANES), F32),
        pltpu.VMEM((layers, 2, tp, ROWS, LANES), F32),
        pltpu.VMEM((layers, 2, tp, ROWS, LANES), F32),
        pltpu.VMEM((layers, 2, tp, ROWS, LANES), F32),
        pltpu.VMEM((layers, rows, columns), BF16),
        pltpu.VMEM((rows, columns), BF16),
        pltpu.VMEM((3, 2, tp + 2, WIDE, LANES), F32),
        pltpu.VMEM((rows, 2 * columns), BF16),
        pltpu.VMEM((4, 2, ROWS, columns), BF16),
        pltpu.VMEM((4, ny * nc, 8, LANES), F32),
        pltpu.VMEM((4, nz, 8, LANES), F32),
        pltpu.VMEM((2, TAPS + 1, LANES), F32),
        pltpu.VMEM((layers, ny * nc, 2, TAPS + 1, LANES), BF16),
        pltpu.VMEM((layers, nz, 2, TAPS + 1, LANES), BF16),
        pltpu.VMEM((layers, 3, ny, nz, nc, piece, columns), BF16),
        pltpu.VMEM((layers, 3, ny, nz, piece, columns), BF16),
        pltpu.VMEM((layers, 3, ny, nz, piece, columns), BF16),
        pltpu.VMEM((layers, ny, 3, nz, piece, columns), BF16),
        pltpu.VMEM((layers, 3, nz, piece, columns), BF16),
        pltpu.VMEM((layers, nz, 3, piece, columns), BF16),
        pltpu.SemaphoreType.DMA((192,)),
        pltpu.SemaphoreType.DMA((192,)),
    ]


def shuffled(rows):
    frames, recs, depth = rows.shape
    return (
        rows.reshape(STREAMS, SEG, recs, depth).transpose(1, 0, 2, 3).reshape(frames * recs, depth)
    )


def restored(rows, recs):
    count, depth = rows.shape
    return (
        rows.reshape(SEG, STREAMS, recs, depth).transpose(1, 0, 2, 3).reshape(count // recs, recs, depth)
    )


def on_device(
    frames,
    lengths,
    value_weight,
    gate_weight,
    tap_weights,
    norm_gain,
    norm_shift,
    project_weight,
    output_grad,
):
    ctx, tp = lax.axis_size("ctx"), lax.axis_size("tp")
    layers, depth, columns = value_weight.shape
    piece = depth // ctx
    vmem = pl.BlockSpec(memory_space=pltpu.VMEM)
    smem = pl.BlockSpec(memory_space=pltpu.SMEM)
    up, value, gate, project, tap = pl.pallas_call(
        functools.partial(fused, ctx, tp),
        out_shape=(
            jax.ShapeDtypeStruct((ROWS, depth), F32),
            jax.ShapeDtypeStruct((layers, piece, columns), F32),
            jax.ShapeDtypeStruct((layers, piece, columns), F32),
            jax.ShapeDtypeStruct((layers, piece, columns), F32),
            jax.ShapeDtypeStruct((layers, TAPS, columns), F32),
        ),
        in_specs=[vmem, vmem, smem, vmem, vmem, vmem, vmem, vmem, vmem],
        out_specs=(vmem,) * 5,
        scratch_shapes=scratch(ctx, tp, layers, depth, columns),
        compiler_params=pltpu.CompilerParams(
            collective_id=0, has_side_effects=True, vmem_limit_bytes=60 * 1024 * 1024
        ),
    )(
        shuffled(frames),
        shuffled(output_grad),
        lengths,
        value_weight,
        gate_weight,
        project_weight,
        tap_weights,
        norm_gain,
        norm_shift,
    )
    return restored(up, frames.shape[1]), value, gate, jnp.swapaxes(project, 1, 2), tap


def solution(mesh):
    in_specs = (
        P(("ctx", "tp"), None, None),
        P(),
        P(None, None, "tp"),
        P(None, None, "tp"),
        P(None, None, "tp"),
        P(None, "tp"),
        P(None, "tp"),
        P(None, "tp", None),
        P(("ctx", "tp"), None, None),
    )
    out_specs = (
        P(("ctx", "tp"), None, None),
        P(None, "ctx", "tp"),
        P(None, "ctx", "tp"),
        P(None, "tp", "ctx"),
        P(None, None, "tp"),
    )
    return jax.shard_map(
        on_device, mesh=mesh, in_specs=in_specs, out_specs=out_specs, check_vma=False
    )
```

```python
import functools

import jax
import jax.numpy as jnp
from jax import lax
from jax.experimental import pallas as pl
from jax.experimental.pallas import tpu as pltpu
from jax.sharding import PartitionSpec as P

EPSILON = 1e-05
MESH = pl.DeviceIdType.MESH
F32, BF16 = jnp.float32, jnp.bfloat16
TAPS, REACH = 31, 15
CHUNK = 32
LANES = 128
STREAMS, SEG = 4, 16
ROWS = SEG * 8
MAIN = REACH * 8
WIDE = (SEG + 2 * REACH) * 8


def grid_of(ctx):
    return {64: (4, 8, 2), 8: (2, 2, 2)}[ctx]


def rows_of(slot, first=0, count=ROWS):
    return pl.ds(pl.multiple_of(slot * ROWS + first, 16), count)


def sigmoid(v):
    return 1.0 / (1.0 + jnp.exp(-v))


def fused(
    ctx,
    tp,
    frames,
    og,
    lengths,
    vw_in,
    gw_in,
    pw_in,
    taps,
    gain,
    shift,
    up_out,
    value_out,
    gate_out,
    project_out,
    tap_out,
    vw,
    gw,
    pw,
    hid,
    up,
    val,
    gath,
    ups,
    part,
    farland,
    land,
    normed,
    lnscale,
    fv,
    fg,
    scaled,
    ds,
    act,
    glu,
    wide,
    lows,
    halo,
    first,
    second,
    tapsum,
    tap1,
    tap2,
    wt,
    in1,
    out2,
    in2,
    out3,
    in3,
    lsem,
    ssem,
    rsem,
):
    ny, nz, nc = grid_of(ctx)
    pos = lax.axis_index("ctx")
    x = lax.axis_index("tp")
    y, z, c = pos // (nz * nc), (pos // nc) % nz, pos % nc
    depth = gath.shape[2]
    columns = value_out.shape[2]

    def to_x(p):
        return {"tp": p}

    def to_yc(p):
        return {"ctx": ((p // nc) * nz + z) * nc + p % nc}

    def to_y(p):
        return {"ctx": (p * nz + z) * nc + c}

    def to_z(p):
        return {"ctx": (y * nz + p) * nc + c}

    def to_c(p):
        return {"ctx": (y * nz + z) * nc + p}

    yc = y * nc + c
    following = {"ctx": lax.rem(pos + 1, ctx)}
    previous = {"ctx": lax.rem(pos + ctx - 1, ctx)}

    barrier = pltpu.get_barrier_semaphore()
    peers = [to_x(lax.rem(x + s, tp)) for s in range(1, tp)]
    peers += [to_yc(lax.rem(yc + s, ny * nc)) for s in range(1, ny * nc)]
    peers += [to_z(lax.rem(z + s, nz)) for s in range(1, nz)]
    peers += [following, previous]
    for peer in peers:
        pl.semaphore_signal(barrier, inc=1, device_id=peer, device_id_type=MESH)
    loads = [
        pltpu.make_async_copy(src, dst, lsem.at[i])
        for i, (src, dst) in enumerate(((vw_in, vw), (gw_in, gw), (pw_in, pw)))
    ]
    for load in loads:
        load.start()

    taken = [0]

    def take(n):
        taken[0] += n
        return taken[0] - n

    def remote(src, dst, send, recv, target):
        return pltpu.make_async_remote_copy(
            src_ref=src,
            dst_ref=dst,
            send_sem=ssem.at[send],
            recv_sem=rsem.at[recv],
            device_id=target,
            device_id_type=MESH,
        )

    class Exchange:
        def __init__(self, count, me, target, src, dst):
            self.count, self.me, self.target, self.src, self.dst = count, me, target, src, dst
            self.base = take(count)
            self.order = list(range(1, count))

        def peer(self, step):
            return lax.rem(self.me + step, self.count)

        def send(self, step):
            p = self.peer(step)
            remote(
                self.src(p), self.dst(self.me), self.base + step, self.base + self.me, self.target(p)
            ).start()

        def start(self):
            for step in self.order:
                self.send(step)

        def landed(self, step):
            p = self.peer(step)
            remote(
                self.src(p), self.dst(p), self.base + step, self.base + p, self.target(p)
            ).wait_recv()

        def sent(self):
            for step in self.order:
                p = self.peer(step)
                remote(
                    self.src(p), self.dst(self.me), self.base + step, self.base + self.me, self.target(p)
                ).wait_send()

        def finish(self):
            for step in self.order:
                self.landed(step)
            self.sent()

    right, left, far = lax.rem(x + 1, tp), lax.rem(x + 3, tp), lax.rem(x + 2, tp)

    class GatherX:
        def __init__(self, buf, which):
            self.rows = lambda d, i: buf.at[which, rows_of(d, i * CHUNK, CHUNK)]
            self.base = take(12)

        def copy(self, owner, i, sem, target):
            ref = self.rows(owner, i)
            return remote(ref, ref, self.base + sem, self.base + sem, to_x(target))

        def push(self, i):
            self.copy(x, i, i, right).start()
            self.copy(x, i, 4 + i, left).start()

        def onward(self, i):
            if i < 2:
                self.copy(left, i, i, right).wait_recv()
                self.copy(left, i, 8 + i, right).start()
            else:
                self.copy(right, i, 4 + i, left).wait_recv()
                self.copy(right, i, 8 + i, left).start()

        def wait_left(self):
            for i in (2, 3):
                self.copy(left, i, i, right).wait_recv()

        def wait_right(self):
            for i in (0, 1):
                self.copy(right, i, 4 + i, left).wait_recv()

        def wait_far(self):
            for i in (0, 2, 1, 3):
                self.copy(far, i, 8 + i, right).wait_recv()

        def sent(self):
            for i in range(4):
                self.copy(x, i, i, right).wait_send()
                self.copy(x, i, 4 + i, left).wait_send()
                if i < 2:
                    self.copy(left, i, 8 + i, right).wait_send()
                else:
                    self.copy(right, i, 8 + i, left).wait_send()

    class ScatterX:
        def __init__(self, u):
            self.u = u
            self.base = take(12)

        def far_copy(self, i):
            return remote(
                part.at[rows_of(far, i * CHUNK, CHUNK)],
                farland.at[self.u, pl.ds(i * CHUNK, CHUNK)],
                self.base + i,
                self.base + i,
                to_x(right if i < 2 else left),
            )

        def near_copy(self, way, i):
            sem = self.base + 4 + 4 * way + i
            return remote(
                part.at[rows_of(left if way else right, i * CHUNK, CHUNK)],
                land.at[self.u, way, pl.ds(i * CHUNK, CHUNK)],
                sem,
                sem,
                to_x(left if way else right),
            )

        def send_far(self):
            for i in (0, 2, 1, 3):
                self.far_copy(i).start()

        def send_early(self):
            self.near_copy(0, 2).start()
            self.near_copy(1, 0).start()

        def send_late(self):
            self.near_copy(0, 3).start()
            self.near_copy(1, 1).start()

        def combine(self, i):
            self.far_copy(i).wait_recv()
            way = 0 if i < 2 else 1
            at = rows_of(left if way else right, i * CHUNK, CHUNK)
            part[at] = (
                part[at].astype(F32) + farland[self.u, i * CHUNK : (i + 1) * CHUNK].astype(F32)
            ).astype(BF16)
            self.near_copy(way, i).start()

        def combine_first(self):
            self.combine(0)
            self.combine(2)

        def combine_last(self):
            self.send_late()
            self.combine(1)
            self.combine(3)

        def landed(self, i):
            self.near_copy(0, i).wait_recv()
            self.near_copy(1, i).wait_recv()

        def sent(self):
            for i in range(4):
                self.far_copy(i).wait_send()
                self.near_copy(0, i).wait_send()
                self.near_copy(1, i).wait_send()

        def rows(self, first_row):
            at = pl.ds(pl.multiple_of(first_row, CHUNK), CHUNK)
            return (
                part[rows_of(x, first_row, CHUNK)].astype(F32)
                + land[self.u, 0, at].astype(F32)
                + land[self.u, 1, at].astype(F32)
            )

    len0, len1 = lengths[0], lengths[1]
    start_frame = pos * (tp * STREAMS * SEG)
    t_in = lax.broadcasted_iota(jnp.int32, (SEG, 8, LANES), 0)
    sub = lax.broadcasted_iota(jnp.int32, (SEG, 8, LANES), 1)
    limit = jnp.where(sub % 2 == 0, len0, len1)
    for s in range(tp):
        frame = start_frame + s * (STREAMS * SEG) + (sub // 2) * SEG + t_in
        val[s] = jnp.where(frame < limit, 1.0, 0.0).astype(F32).reshape(ROWS, LANES)
    span = tp * STREAMS * SEG
    total = (len0 + len1).astype(F32)
    local_count = (
        jnp.clip(len0 - start_frame, 0, span) + jnp.clip(len1 - start_frame, 0, span)
    ).astype(F32)

    def halves(h):
        return slice(h * LANES, (h + 1) * LANES)

    def reduce_tile(u, rows, merge, meanwhile=None, later=None):
        first[u, yc] = jnp.zeros((8, LANES), F32)
        for i, row in enumerate(rows):
            first[u, yc, i : i + 1, :] = row
        one = Exchange(
            ny * nc, yc, to_yc, lambda p: first.at[u, yc], lambda p: first.at[u, p]
        )
        one.start()
        if meanwhile is not None:
            meanwhile()
        one.finish()
        second[u, z] = merge([first[u, i] for i in range(ny * nc)])
        two = Exchange(nz, z, to_z, lambda p: second.at[u, z], lambda p: second.at[u, p])
        two.start()
        if later is not None:
            later()
        two.finish()
        return merge([second[u, i] for i in range(nz)])

    def merge_sum(tiles):
        whole = tiles[0]
        for tile in tiles[1:]:
            whole = whole + tile
        return whole

    def merge_moments(tiles):
        whole = merge_sum(tiles)
        mean = whole[0:2] / jnp.maximum(whole[4:5], 1.0)
        square = whole[2:4]
        for tile in tiles:
            gap = tile[0:2] / jnp.maximum(tile[4:5], 1.0) - mean
            square = square + tile[4:5] * gap * gap
        return jnp.concatenate([whole[0:2], square, whole[4:8]], axis=0)

    def fold(v):
        return jnp.sum(v.reshape(SEG, 8, LANES), axis=0)

    tile_sub = lax.broadcasted_iota(jnp.int32, (REACH, 8, LANES), 1)

    def widen(e, s):
        for h in range(2):
            cur = wide[e, h, s, MAIN + 8 : MAIN + ROWS].reshape(REACH, 8, LANES)
            old = wide[e, h, s - 1, MAIN + 8 : MAIN + ROWS].reshape(REACH, 8, LANES)
            low = jnp.where(tile_sub < 2, pltpu.roll(old, 2, 1), pltpu.roll(cur, 2, 1))
            wide[e, h, s, 0:MAIN] = low.reshape(MAIN, LANES)
            cur = wide[e, h, s, MAIN : MAIN + ROWS - 8].reshape(REACH, 8, LANES)
            new = wide[e, h, s + 1, MAIN : MAIN + ROWS - 8].reshape(REACH, 8, LANES)
            high = jnp.where(tile_sub >= 6, pltpu.roll(new, 6, 1), pltpu.roll(cur, 6, 1))
            wide[e, h, s, MAIN + ROWS : WIDE] = high.reshape(MAIN, LANES)

    def convolve(e, layer, h, s, forward):
        result = None
        for j in range(TAPS):
            at = (j if forward else TAPS - 1 - j) * 8
            term = taps[j, layer : layer + 1, halves(h)] * wide[e, h, s, at : at + ROWS]
            result = term if result is None else result + term
        return result

    class Halo:
        def __init__(self, u):
            self.u = u
            base = take(2)
            self.up = remote(
                glu.at[rows_of(tp - 1)], halo.at[u, 0], base, base, following
            )
            self.down = remote(glu.at[rows_of(0)], halo.at[u, 1], base + 1, base + 1, previous)

        def start(self):
            self.up.start()
            self.down.start()

        def finish(self, e):
            self.up.wait()
            self.down.wait()
            has_low = (pos > 0).astype(F32)
            has_high = (pos < ctx - 1).astype(F32)
            for h in range(2):
                wide[e, h, 0, MAIN : MAIN + ROWS] = halo[self.u, 0, :, halves(h)].astype(F32) * has_low
                wide[e, h, tp + 1, MAIN : MAIN + ROWS] = (
                    halo[self.u, 1, :, halves(h)].astype(F32) * has_high
                )

    class Scatter:
        def __init__(self, layer, low, high):
            self.layer, self.low, self.high = layer, low, high
            other = lax.rem(c + 1, nc)
            base = take(1)
            mats = slice(low, high)
            self.core = remote(
                wt.at[layer, mats, :, :, other], in1.at[layer, mats], base, base, to_c(other)
            )
            self.ys = Exchange(
                ny, y, to_y, lambda p: out2.at[layer, mats, p], lambda p: in2.at[layer, p, mats]
            )
            self.zs = Exchange(
                nz, z, to_z, lambda p: out3.at[layer, mats, p], lambda p: in3.at[layer, p, mats]
            )

        def start(self):
            self.core.start()

        def after_core(self):
            layer = self.layer
            self.core.wait()

            def add(i, carry):
                a, b = i // ny, i % ny
                out2[layer, a, b] = (
                    wt[layer, a, b, :, c].astype(F32) + in1[layer, a, b].astype(F32)
                ).astype(BF16)
                return carry

            lax.fori_loop(self.low * ny, self.high * ny, add, 0)
            self.ys.start()

        def after_y(self):
            layer = self.layer
            self.ys.finish()

            def add(a, carry):
                whole = out2[layer, a, y].astype(F32)
                for s in range(1, ny):
                    whole = whole + in2[layer, lax.rem(y + s, ny), a].astype(F32)
                out3[layer, a] = whole.astype(BF16)
                return carry

            lax.fori_loop(self.low, self.high, add, 0)
            self.zs.start()

        def after_z(self):
            layer = self.layer
            self.zs.finish()
            outs = (value_out, gate_out, project_out)
            for a, out in list(enumerate(outs))[self.low : self.high]:
                whole = out3[layer, a, z].astype(F32)
                for s in range(1, nz):
                    whole = whole + in3[layer, lax.rem(z + s, nz), a].astype(F32)
                out[layer] = whole

    def weight_term(left, right, put):
        def step(i, carry):
            cols = pl.ds(pl.multiple_of(i * (depth // ny), depth // ny), depth // ny)
            whole = lax.dot_general(
                left[:, cols], right[...], (((0,), (0,)), ((), ())), preferred_element_type=F32
            )
            put(i, whole.astype(BF16))
            return carry

        lax.fori_loop(0, ny, step, 0)

    class TapSum:
        def __init__(self, layer):
            self.layer = layer
            self.one = Exchange(
                ny * nc, yc, to_yc, lambda p: tap1.at[layer, yc], lambda p: tap1.at[layer, p]
            )
            self.two = Exchange(
                nz, z, to_z, lambda p: tap2.at[layer, z], lambda p: tap2.at[layer, p]
            )

        def start(self):
            tap1[self.layer, yc] = tapsum[...].astype(BF16)
            self.one.start()

        def middle(self):
            self.one.finish()
            whole = tap1[self.layer, 0].astype(F32)
            for i in range(1, ny * nc):
                whole = whole + tap1[self.layer, i].astype(F32)
            tap2[self.layer, z] = whole.astype(BF16)
            self.two.start()

        def finish(self):
            self.two.finish()
            whole = tap2[self.layer, 0].astype(F32)
            for i in range(1, nz):
                whole = whole + tap2[self.layer, i].astype(F32)
            for h in range(2):
                tap_out[:, self.layer, halves(h)] = whole[h, 0:TAPS]

    def pair(group, step):
        lax.fori_loop(0, 2, lambda k, carry: step((2 * k + group) * CHUNK) or carry, 0)

    def tiles(first_row):
        return pl.ds(first_row // 8, CHUNK // 8)

    def rows_in(ref, first_row):
        return ref[tiles(first_row)].reshape(CHUNK, depth)

    def fill(src, dst):
        def step(t, carry):
            for q in range(STREAMS):
                dst[t, 2 * q : 2 * q + 2, :] = src[q, t].astype(F32)
            return carry

        lax.fori_loop(0, SEG, step, 0)

    def normalize(layer, rows_at, first_row):
        at = pl.ds(pl.multiple_of(first_row, CHUNK), CHUNK)
        rows = rows_at(first_row)
        centered = rows - jnp.mean(rows, axis=1, keepdims=True)
        scale = lax.rsqrt(jnp.mean(centered * centered, axis=1, keepdims=True) + EPSILON)
        out = centered * scale
        normed[layer, at] = out
        lnscale[layer, at] = jnp.broadcast_to(scale, (CHUNK, LANES))
        gath[layer, rows_of(x, first_row, CHUNK)] = out.astype(BF16)

    def back_rows(layer, summed, first_row):
        at = pl.ds(pl.multiple_of(first_row, CHUNK), CHUNK)
        grad = summed.rows(first_row)
        unit = normed[layer, at]
        cross = jnp.mean(grad * unit, axis=1, keepdims=True)
        scale = lnscale[layer, at][:, 0:1]
        return scale * (grad - jnp.mean(grad, axis=1, keepdims=True) - unit * cross)

    def forward(layer, gather, after, later):
        def block(s):
            rows = gath[layer, rows_of(s)]
            value = jnp.dot(rows, vw[layer], preferred_element_type=F32)
            gate = sigmoid(jnp.dot(rows, gw[layer], preferred_element_type=F32))
            for h in range(2):
                v, g = value[:, halves(h)], gate[:, halves(h)]
                keep = g * val[s]
                fv[layer, h, s] = keep
                fg[layer, h, s] = v * (1.0 - g) * keep
                low = (v * keep).astype(BF16)
                glu[rows_of(s), halves(h)] = low
                wide[layer, h, s + 1, MAIN : MAIN + ROWS] = low.astype(F32)

        gather.onward(0)
        gather.onward(2)
        block(x)
        gather.onward(1)
        gather.onward(3)
        after()
        gather.wait_left()
        block(left)
        gather.wait_right()
        block(right)
        gather.wait_far()
        block(far)
        edge = Halo(layer)
        edge.start()

        def conv(s, carry):
            widen(layer, s + 1)
            sums = []
            for h in range(2):
                mixed = convolve(layer, layer, h, s + 1, True)
                scaled[layer, h, s] = mixed
                sums.append(carry[h] + fold(mixed * val[s]))
            return tuple(sums)

        zero = jnp.zeros((8, LANES), F32)
        sums = lax.fori_loop(1, tp - 1, conv, (zero, zero))
        edge.finish(layer)
        sums = lax.fori_loop(0, 2, lambda i, carry: conv(i * (tp - 1), carry), sums)
        sums = [jnp.sum(v, axis=0, keepdims=True) for v in sums]
        means = [v / jnp.maximum(local_count, 1.0) for v in sums]

        def spread(s, carry):
            out = []
            for h in range(2):
                gap = (scaled[layer, h, s] - means[h]) * val[s]
                out.append(carry[h] + fold(gap * gap))
            return tuple(out)

        squares = lax.fori_loop(0, tp, spread, (zero, zero))
        squares = [jnp.sum(v, axis=0, keepdims=True) for v in squares]
        count = jnp.zeros((1, LANES), F32) + local_count
        whole = reduce_tile(layer, sums + squares + [count], merge_moments, gather.sent, later)
        mean = [whole[h : h + 1] / total for h in range(2)]
        scale = [lax.rsqrt(whole[2 + h : 3 + h] / total + EPSILON) for h in range(2)]

        def activate(s):
            for h in range(2):
                unit = (scaled[layer, h, s] - mean[h]) * scale[h]
                shifted = gain[layer : layer + 1, halves(h)] * unit + shift[layer : layer + 1, halves(h)]
                sig = sigmoid(shifted)
                keep = sig * val[s]
                scaled[layer, h, s] = unit
                ds[layer, h, s] = keep * (1.0 + shifted * (1.0 - sig))
                act[layer, rows_of(s), halves(h)] = (shifted * keep).astype(BF16)

        return activate, scale

    def backward(layer, u, up_block, chan_scale, activate, between, after_send, weights_first):
        zero = jnp.zeros((8, LANES), F32)

        def one_block(s, carry):
            if activate is not None:
                activate(s)
            grad = lax.dot_general(
                ups[layer, rows_of(s)], pw[layer], (((1,), (1,)), ((), ())), preferred_element_type=F32
            )
            sums = list(carry)
            for h in range(2):
                g = grad[:, halves(h)] * ds[layer, h, s]
                ds[layer, h, s] = g
                sums[h] = sums[h] + fold(g)
                sums[2 + h] = sums[2 + h] + fold(g * scaled[layer, h, s])
            return tuple(sums)

        sums = up_block(one_block, (zero,) * 4)
        sums = [jnp.sum(v, axis=0, keepdims=True) for v in sums]

        scatters = [Scatter(layer, 2, 3), Scatter(layer, 0, 2)] if weights_first else [Scatter(layer, 0, 3)]

        def project():
            def put(i, block):
                wt[layer, 2, i] = block.reshape(wt.shape[3:])

            weight_term(ups.at[layer], act.at[layer], put)
            if weights_first:
                scatters[0].start()

        whole = reduce_tile(2 + layer, sums, merge_sum, project)
        if weights_first:
            scatters[0].after_core()

        def mix(s, carry):
            for h in range(2):
                factor = gain[layer : layer + 1, halves(h)] * chan_scale[h]
                a, b = whole[h : h + 1] / total, whole[2 + h : 3 + h] / total
                grad = factor * (ds[layer, h, s] - a - scaled[layer, h, s] * b) * val[s]
                wide[2, h, s + 1, MAIN : MAIN + ROWS] = grad
                glu[rows_of(s), halves(h)] = grad.astype(BF16)
            return carry

        lax.fori_loop(0, tp, mix, 0)
        edge = Halo(2 + layer)
        edge.start()

        def tap(j, carry):
            at = pl.ds(pl.multiple_of(j * 8, 8), ROWS)
            for h in range(2):
                whole = None
                for s in range(1, tp + 1):
                    term = fold(wide[layer, h, s, at] * wide[2, h, s, MAIN : MAIN + ROWS])
                    whole = term if whole is None else whole + term
                tapsum[h, pl.ds(j, 1), :] = jnp.sum(whole, axis=0, keepdims=True)
            return carry

        lax.fori_loop(0, TAPS, tap, 0)
        tap_total = TapSum(layer)
        edge.finish(2)
        tap_total.start()
        between()
        if weights_first:
            scatters[0].after_y()

        send = ScatterX(u)

        def lows_block(s):
            widen(2, s + 1)
            for h in range(2):
                grad = convolve(2, layer, h, s + 1, False)
                lows[rows_of(s), halves(h)] = (grad * fv[layer, h, s]).astype(BF16)
                lows[rows_of(s), slice(columns + h * LANES, columns + (h + 1) * LANES)] = (
                    grad * fg[layer, h, s]
                ).astype(BF16)

        def grad_block(s):
            whole = lax.dot_general(
                lows[rows_of(s), 0:columns],
                vw[layer],
                (((1,), (1,)), ((), ())),
                preferred_element_type=F32,
            ) + lax.dot_general(
                lows[rows_of(s), columns : 2 * columns],
                gw[layer],
                (((1,), (1,)), ((), ())),
                preferred_element_type=F32,
            )
            part[rows_of(s)] = whole.astype(BF16)

        def put(i, block):
            wt[layer, 0, i] = block[:, 0:columns].reshape(wt.shape[3:])
            wt[layer, 1, i] = block[:, columns:].reshape(wt.shape[3:])

        def weights():
            weight_term(gath.at[layer], lows, put)
            scatters[-1].start()

        def block(s):
            if not weights_first:
                lows_block(s)
            grad_block(s)

        if weights_first:
            lax.fori_loop(0, tp, lambda s, carry: lows_block(s) or carry, 0)
            weights()
        block(far)
        send.send_far()
        block(right)
        block(left)
        send.send_early()
        block(x)
        after_send(scatters, tap_total)
        send.combine_first()
        send.combine_last()
        if not weights_first:
            weights()
        return send, scatters, tap_total

    tapsum[...] = jnp.zeros(tapsum.shape, F32)
    fill(frames, hid)
    gather = GatherX(gath, 0)
    for group in (0, 1):
        pair(group, lambda first_row: normalize(0, lambda r: rows_in(hid, r), first_row))
    pl.semaphore_wait(barrier, len(peers))
    for i in (0, 2, 1, 3):
        gather.push(i)
    fill(og, up)
    gather_up = GatherX(ups, 1)

    def copy_up(first_row):
        ups[1, rows_of(x, first_row, CHUNK)] = rows_in(up, first_row).astype(BF16)

    for group in (0, 1):
        pair(group, copy_up)
    for load in loads:
        load.wait()

    def send_up():
        for i in (0, 2, 1, 3):
            gather_up.push(i)

    def up_onward():
        for i in (0, 2, 1, 3):
            gather_up.onward(i)

    activate, scale0 = forward(0, gather, send_up, up_onward)
    branch = ScatterX(0)

    def project_block(s):
        activate(s)
        part[rows_of(s)] = jnp.dot(
            act[0, rows_of(s)], pw[0], preferred_element_type=F32
        ).astype(BF16)

    project_block(far)
    branch.send_far()
    project_block(right)
    project_block(left)
    branch.send_early()
    project_block(x)
    branch.combine_first()
    branch.combine_last()

    def hidden(first_row):
        return (rows_in(hid, first_row) + branch.rows(first_row)).astype(BF16).astype(F32)

    gather = GatherX(gath, 1)
    for group in (0, 1):
        branch.landed(group)
        branch.landed(group + 2)
        pair(group, lambda first_row: normalize(1, hidden, first_row))
        gather.push(group)
        gather.push(group + 2)
    branch.sent()

    def nothing():
        return None

    activate, scale1 = forward(1, gather, nothing, None)
    gather_up.wait_left()
    gather_up.wait_right()
    gather_up.wait_far()
    gather_up.sent()

    def all_blocks(block, carry):
        return lax.fori_loop(0, tp, block, carry)

    send, (scatter1,), taps1 = backward(
        1, 1, all_blocks, scale1, activate, nothing, lambda scatters, tap_total: tap_total.middle(), False
    )
    gather0 = GatherX(ups, 0)

    def next_up(first_row):
        whole = rows_in(up, first_row) + back_rows(1, send, first_row)
        up[tiles(first_row)] = whole.reshape(CHUNK // 8, 8, depth)
        ups[0, rows_of(x, first_row, CHUNK)] = whole.astype(BF16)

    for group in (0, 1):
        send.landed(group)
        send.landed(group + 2)
        pair(group, next_up)
        gather0.push(group)
        gather0.push(group + 2)

    def in_turn(block, carry):
        gather0.onward(0)
        gather0.onward(2)
        carry = block(x, carry)
        gather0.onward(1)
        gather0.onward(3)
        scatter1.after_core()
        send.sent()
        taps1.finish()
        gather0.wait_left()
        carry = block(left, carry)
        gather0.wait_right()
        carry = block(right, carry)
        gather0.wait_far()
        carry = block(far, carry)
        gather0.sent()
        return carry

    def finish_first(scatters, tap_total):
        tap_total.middle()
        scatters[0].after_z()
        scatter1.after_z()
        scatters[1].after_core()

    last, scatters0, taps0 = backward(
        0, 2, in_turn, scale0, None, scatter1.after_y, finish_first, True
    )

    def last_up(first_row):
        whole = rows_in(up, first_row) + back_rows(0, last, first_row)
        up[tiles(first_row)] = whole.reshape(CHUNK // 8, 8, depth)

        def put(i, carry):
            t = first_row // 8 + i
            for q in range(STREAMS):
                up_out[q, t] = up[t, 2 * q : 2 * q + 2, :]
            return carry

        lax.fori_loop(0, CHUNK // 8, put, 0)

    for group in (0, 1):
        last.landed(group)
        last.landed(group + 2)
        pair(group, last_up)
    last.sent()
    scatters0[1].after_y()
    taps0.finish()
    scatters0[1].after_z()


def scratch(ctx, tp, layers, depth, columns):
    ny, nz, nc = grid_of(ctx)
    rows = tp * ROWS
    piece = depth // ctx
    return [
        pltpu.VMEM((layers, depth, columns), BF16),
        pltpu.VMEM((layers, depth, columns), BF16),
        pltpu.VMEM((layers, columns, depth), BF16),
        pltpu.VMEM((SEG, 8, depth), F32),
        pltpu.VMEM((SEG, 8, depth), F32),
        pltpu.VMEM((tp, ROWS, LANES), F32),
        pltpu.VMEM((layers, rows, depth), BF16),
        pltpu.VMEM((layers, rows, depth), BF16),
        pltpu.VMEM((rows, depth), BF16),
        pltpu.VMEM((3, ROWS, depth), BF16),
        pltpu.VMEM((3, 2, ROWS, depth), BF16),
        pltpu.VMEM((layers, ROWS, depth), F32),
        pltpu.VMEM((layers, ROWS, LANES), F32),
        pltpu.VMEM((layers, 2, tp, ROWS, LANES), F32),
        pltpu.VMEM((layers, 2, tp, ROWS, LANES), F32),
        pltpu.VMEM((layers, 2, tp, ROWS, LANES), F32),
        pltpu.VMEM((layers, 2, tp, ROWS, LANES), F32),
        pltpu.VMEM((layers, rows, columns), BF16),
        pltpu.VMEM((rows, columns), BF16),
        pltpu.VMEM((3, 2, tp + 2, WIDE, LANES), F32),
        pltpu.VMEM((rows, 2 * columns), BF16),
        pltpu.VMEM((4, 2, ROWS, columns), BF16),
        pltpu.VMEM((4, ny * nc, 8, LANES), F32),
        pltpu.VMEM((4, nz, 8, LANES), F32),
        pltpu.VMEM((2, TAPS + 1, LANES), F32),
        pltpu.VMEM((layers, ny * nc, 2, TAPS + 1, LANES), BF16),
        pltpu.VMEM((layers, nz, 2, TAPS + 1, LANES), BF16),
        pltpu.VMEM((layers, 3, ny, nz, nc, piece, columns), BF16),
        pltpu.VMEM((layers, 3, ny, nz, piece, columns), BF16),
        pltpu.VMEM((layers, 3, ny, nz, piece, columns), BF16),
        pltpu.VMEM((layers, ny, 3, nz, piece, columns), BF16),
        pltpu.VMEM((layers, 3, nz, piece, columns), BF16),
        pltpu.VMEM((layers, nz, 3, piece, columns), BF16),
        pltpu.SemaphoreType.DMA((3,)),
        pltpu.SemaphoreType.DMA((256,)),
        pltpu.SemaphoreType.DMA((256,)),
    ]


def on_device(
    frames,
    lengths,
    value_weight,
    gate_weight,
    tap_weights,
    norm_gain,
    norm_shift,
    project_weight,
    output_grad,
):
    ctx, tp = lax.axis_size("ctx"), lax.axis_size("tp")
    layers, depth, columns = value_weight.shape
    piece = depth // ctx
    vmem = pl.BlockSpec(memory_space=pltpu.VMEM)
    smem = pl.BlockSpec(memory_space=pltpu.SMEM)
    hbm = pl.BlockSpec(memory_space=pl.ANY)
    recs = frames.shape[1]
    split = (STREAMS, SEG, recs, depth)
    up, value, gate, project, tap = pl.pallas_call(
        functools.partial(fused, ctx, tp),
        out_shape=(
            jax.ShapeDtypeStruct(split, F32),
            jax.ShapeDtypeStruct((layers, piece, columns), F32),
            jax.ShapeDtypeStruct((layers, piece, columns), F32),
            jax.ShapeDtypeStruct((layers, piece, columns), F32),
            jax.ShapeDtypeStruct((TAPS, layers, columns), F32),
        ),
        in_specs=[vmem, vmem, smem, hbm, hbm, hbm, vmem, vmem, vmem],
        out_specs=(vmem,) * 5,
        scratch_shapes=scratch(ctx, tp, layers, depth, columns),
        compiler_params=pltpu.CompilerParams(
            collective_id=0, has_side_effects=True, vmem_limit_bytes=60 * 1024 * 1024
        ),
    )(
        frames.reshape(split),
        output_grad.reshape(split),
        lengths,
        value_weight,
        gate_weight,
        project_weight,
        jnp.swapaxes(tap_weights, 0, 1),
        norm_gain,
        norm_shift,
    )
    return (
        up.reshape(frames.shape),
        value,
        gate,
        jnp.swapaxes(project, 1, 2),
        jnp.swapaxes(tap, 0, 1),
    )


def solution(mesh):
    in_specs = (
        P(("ctx", "tp"), None, None),
        P(),
        P(None, None, "tp"),
        P(None, None, "tp"),
        P(None, None, "tp"),
        P(None, "tp"),
        P(None, "tp"),
        P(None, "tp", None),
        P(("ctx", "tp"), None, None),
    )
    out_specs = (
        P(("ctx", "tp"), None, None),
        P(None, "ctx", "tp"),
        P(None, "ctx", "tp"),
        P(None, "tp", "ctx"),
        P(None, None, "tp"),
    )
    return jax.shard_map(
        on_device, mesh=mesh, in_specs=in_specs, out_specs=out_specs, check_vma=False
    )
```

```python
import functools

import jax
import jax.numpy as jnp
from jax import lax
from jax.experimental import pallas as pl
from jax.experimental.pallas import tpu as pltpu
from jax.sharding import PartitionSpec as P

EPSILON = 1e-05
MESH = pl.DeviceIdType.MESH
F32, BF16 = jnp.float32, jnp.bfloat16
TAPS, REACH = 31, 15
CHUNK = 32
LANES = 128
STREAMS, SEG = 4, 16
ROWS = SEG * 8
MAIN = REACH * 8
WIDE = (SEG + 2 * REACH) * 8


def grid_of(ctx):
    return {64: (4, 8, 2), 8: (2, 2, 2)}[ctx]


def rows_of(slot, first=0, count=ROWS):
    return pl.ds(pl.multiple_of(slot * ROWS + first, 16), count)


def sigmoid(v):
    return 1.0 / (1.0 + jnp.exp(-v))


def fused(
    ctx,
    tp,
    frames,
    og,
    lengths,
    vw_in,
    gw_in,
    pw_in,
    taps,
    gain,
    shift,
    up_out,
    value_out,
    gate_out,
    project_out,
    tap_out,
    vw,
    gw,
    pw,
    hid,
    up,
    val,
    gath,
    ups,
    part,
    farland,
    land,
    normed,
    lnscale,
    fv,
    fg,
    scaled,
    ds,
    act,
    glu,
    wide,
    lows,
    halo,
    halo2,
    first,
    second,
    tapsum,
    tap1,
    tap2,
    wt,
    in1,
    out2,
    in2,
    out3,
    in3,
    in2z,
    out3z,
    in3z,
    lsem,
    ssem,
    rsem,
):
    ny, nz, nc = grid_of(ctx)
    pos = lax.axis_index("ctx")
    x = lax.axis_index("tp")
    y, z, c = pos // (nz * nc), (pos // nc) % nz, pos % nc
    depth = gath.shape[2]
    columns = value_out.shape[2]

    def to_x(p):
        return {"tp": p}

    def to_yc(p):
        return {"ctx": ((p // nc) * nz + z) * nc + p % nc}

    def to_y(p):
        return {"ctx": (p * nz + z) * nc + c}

    def to_z(p):
        return {"ctx": (y * nz + p) * nc + c}

    def to_c(p):
        return {"ctx": (y * nz + z) * nc + p}

    yc = y * nc + c
    following = {"ctx": lax.rem(pos + 1, ctx)}
    previous = {"ctx": lax.rem(pos + ctx - 1, ctx)}

    barrier = pltpu.get_barrier_semaphore()
    peers = [to_x(lax.rem(x + s, tp)) for s in range(1, tp)]
    peers += [to_yc(lax.rem(yc + s, ny * nc)) for s in range(1, ny * nc)]
    peers += [to_z(lax.rem(z + s, nz)) for s in range(1, nz)]
    peers += [following, previous]
    for peer in peers:
        pl.semaphore_signal(barrier, inc=1, device_id=peer, device_id_type=MESH)
    loads = [
        pltpu.make_async_copy(src, dst, lsem.at[i])
        for i, (src, dst) in enumerate(((vw_in, vw), (gw_in, gw), (pw_in, pw)))
    ]
    for load in loads:
        load.start()

    taken = [0]

    def take(n):
        taken[0] += n
        return taken[0] - n

    def remote(src, dst, send, recv, target):
        return pltpu.make_async_remote_copy(
            src_ref=src,
            dst_ref=dst,
            send_sem=ssem.at[send],
            recv_sem=rsem.at[recv],
            device_id=target,
            device_id_type=MESH,
        )

    class Exchange:
        def __init__(self, count, me, target, src, dst):
            self.count, self.me, self.target, self.src, self.dst = count, me, target, src, dst
            self.base = take(count)
            self.order = list(range(1, count))

        def peer(self, step):
            return lax.rem(self.me + step, self.count)

        def send(self, step):
            p = self.peer(step)
            remote(
                self.src(p), self.dst(self.me), self.base + step, self.base + self.me, self.target(p)
            ).start()

        def start(self):
            for step in self.order:
                self.send(step)

        def landed(self, step):
            p = self.peer(step)
            remote(
                self.src(p), self.dst(p), self.base + step, self.base + p, self.target(p)
            ).wait_recv()

        def sent(self):
            for step in self.order:
                p = self.peer(step)
                remote(
                    self.src(p), self.dst(self.me), self.base + step, self.base + self.me, self.target(p)
                ).wait_send()

        def finish(self):
            for step in self.order:
                self.landed(step)
            self.sent()

    right, left, far = lax.rem(x + 1, tp), lax.rem(x + 3, tp), lax.rem(x + 2, tp)

    class GatherX:
        def __init__(self, buf, which):
            self.rows = lambda d, i: buf.at[which, rows_of(d, i * CHUNK, CHUNK)]
            self.base = take(12)

        def copy(self, owner, i, sem, target):
            ref = self.rows(owner, i)
            return remote(ref, ref, self.base + sem, self.base + sem, to_x(target))

        def push(self, i):
            self.copy(x, i, i, right).start()
            self.copy(x, i, 4 + i, left).start()

        def onward(self, i):
            if i < 2:
                self.copy(left, i, i, right).wait_recv()
                self.copy(left, i, 8 + i, right).start()
            else:
                self.copy(right, i, 4 + i, left).wait_recv()
                self.copy(right, i, 8 + i, left).start()

        def wait_left(self):
            for i in (2, 3):
                self.copy(left, i, i, right).wait_recv()

        def wait_right(self):
            for i in (0, 1):
                self.copy(right, i, 4 + i, left).wait_recv()

        def wait_far(self):
            for i in (0, 2, 1, 3):
                self.copy(far, i, 8 + i, right).wait_recv()

        def sent(self):
            for i in range(4):
                self.copy(x, i, i, right).wait_send()
                self.copy(x, i, 4 + i, left).wait_send()
                if i < 2:
                    self.copy(left, i, 8 + i, right).wait_send()
                else:
                    self.copy(right, i, 8 + i, left).wait_send()

    class ScatterX:
        def __init__(self, u):
            self.u = u
            self.base = take(12)

        def far_copy(self, i):
            return remote(
                part.at[rows_of(far, i * CHUNK, CHUNK)],
                farland.at[self.u, pl.ds(i * CHUNK, CHUNK)],
                self.base + i,
                self.base + i,
                to_x(right if i < 2 else left),
            )

        def near_copy(self, way, i):
            sem = self.base + 4 + 4 * way + i
            return remote(
                part.at[rows_of(left if way else right, i * CHUNK, CHUNK)],
                land.at[self.u, way, pl.ds(i * CHUNK, CHUNK)],
                sem,
                sem,
                to_x(left if way else right),
            )

        def send_far(self):
            for i in (0, 2, 1, 3):
                self.far_copy(i).start()

        def send_early(self):
            self.near_copy(0, 2).start()
            self.near_copy(1, 0).start()

        def send_late(self):
            self.near_copy(0, 3).start()
            self.near_copy(1, 1).start()

        def combine(self, i):
            self.far_copy(i).wait_recv()
            way = 0 if i < 2 else 1
            at = rows_of(left if way else right, i * CHUNK, CHUNK)
            part[at] = (
                part[at].astype(F32) + farland[self.u, i * CHUNK : (i + 1) * CHUNK].astype(F32)
            ).astype(BF16)
            self.near_copy(way, i).start()

        def combine_first(self):
            self.combine(0)
            self.combine(2)

        def combine_last(self):
            self.send_late()
            self.combine(1)
            self.combine(3)

        def landed(self, i):
            self.near_copy(0, i).wait_recv()
            self.near_copy(1, i).wait_recv()

        def sent(self):
            for i in range(4):
                self.far_copy(i).wait_send()
                self.near_copy(0, i).wait_send()
                self.near_copy(1, i).wait_send()

        def rows(self, first_row):
            at = pl.ds(pl.multiple_of(first_row, CHUNK), CHUNK)
            return (
                part[rows_of(x, first_row, CHUNK)].astype(F32)
                + land[self.u, 0, at].astype(F32)
                + land[self.u, 1, at].astype(F32)
            )

    len0, len1 = lengths[0], lengths[1]
    start_frame = pos * (tp * STREAMS * SEG)
    t_in = lax.broadcasted_iota(jnp.int32, (SEG, 8, LANES), 0)
    sub = lax.broadcasted_iota(jnp.int32, (SEG, 8, LANES), 1)
    limit = jnp.where(sub % 2 == 0, len0, len1)
    for s in range(-1, tp + 1):
        frame = start_frame + s * (STREAMS * SEG) + (sub // 2) * SEG + t_in
        val[tp + 1 if s == tp else s if s >= 0 else tp] = jnp.where(frame < limit, 1.0, 0.0).astype(F32).reshape(ROWS, LANES)
    span = tp * STREAMS * SEG
    total = (len0 + len1).astype(F32)
    local_count = (
        jnp.clip(len0 - start_frame, 0, span) + jnp.clip(len1 - start_frame, 0, span)
    ).astype(F32)

    def halves(h):
        return slice(h * LANES, (h + 1) * LANES)

    def reduce_tile(u, rows, merge, meanwhile=None, later=None):
        first[u, yc] = jnp.zeros((8, LANES), F32)
        for i, row in enumerate(rows):
            first[u, yc, i : i + 1, :] = row
        one = Exchange(
            ny * nc, yc, to_yc, lambda p: first.at[u, yc], lambda p: first.at[u, p]
        )
        one.start()
        if meanwhile is not None:
            meanwhile()
        one.finish()
        second[u, z] = merge([first[u, i] for i in range(ny * nc)])
        two = Exchange(nz, z, to_z, lambda p: second.at[u, z], lambda p: second.at[u, p])
        two.start()
        if later is not None:
            later()
        two.finish()
        return merge([second[u, i] for i in range(nz)])

    def merge_sum(tiles):
        whole = tiles[0]
        for tile in tiles[1:]:
            whole = whole + tile
        return whole

    def merge_moments(tiles):
        whole = merge_sum(tiles)
        mean = whole[0:2] / jnp.maximum(whole[4:5], 1.0)
        square = whole[2:4]
        for tile in tiles:
            gap = tile[0:2] / jnp.maximum(tile[4:5], 1.0) - mean
            square = square + tile[4:5] * gap * gap
        return jnp.concatenate([whole[0:2], square, whole[4:8]], axis=0)

    def fold(v):
        return jnp.sum(v.reshape(SEG, 8, LANES), axis=0)

    tile_sub = lax.broadcasted_iota(jnp.int32, (REACH, 8, LANES), 1)

    def widen(e, s):
        for h in range(2):
            cur = wide[e, h, s, MAIN + 8 : MAIN + ROWS].reshape(REACH, 8, LANES)
            old = wide[e, h, s - 1, MAIN + 8 : MAIN + ROWS].reshape(REACH, 8, LANES)
            low = jnp.where(tile_sub < 2, pltpu.roll(old, 2, 1), pltpu.roll(cur, 2, 1))
            wide[e, h, s, 0:MAIN] = low.reshape(MAIN, LANES)
            cur = wide[e, h, s, MAIN : MAIN + ROWS - 8].reshape(REACH, 8, LANES)
            new = wide[e, h, s + 1, MAIN : MAIN + ROWS - 8].reshape(REACH, 8, LANES)
            high = jnp.where(tile_sub >= 6, pltpu.roll(new, 6, 1), pltpu.roll(cur, 6, 1))
            wide[e, h, s, MAIN + ROWS : WIDE] = high.reshape(MAIN, LANES)

    def convolve(e, layer, h, s, forward):
        result = None
        for j in range(TAPS):
            at = (j if forward else TAPS - 1 - j) * 8
            term = taps[j, layer : layer + 1, halves(h)] * wide[e, h, s, at : at + ROWS]
            result = term if result is None else result + term
        return result

    class Halo:
        def __init__(self, u, src, dst):
            self.u = u
            base = take(2)
            self.up = remote(src.at[rows_of(tp - 1)], dst.at[u, 0], base, base, following)
            self.down = remote(src.at[rows_of(0)], dst.at[u, 1], base + 1, base + 1, previous)

        def start(self):
            self.up.start()
            self.down.start()

        def wait(self):
            self.up.wait()
            self.down.wait()

    has_low = (pos > 0).astype(F32)
    has_high = (pos < ctx - 1).astype(F32)

    class Scatter:
        def __init__(self, layer, low, high):
            self.layer, self.low, self.high = layer, low, high
            other = lax.rem(c + 1, nc)
            base = take(1)
            mats = slice(low, high)
            self.core = remote(
                wt.at[layer, mats, :, :, other], in1.at[layer, mats], base, base, to_c(other)
            )
            self.ys = Exchange(
                ny, y, to_y, lambda p: out2.at[layer, mats, p], lambda p: in2.at[layer, p, mats]
            )
            self.zs = Exchange(
                nz, z, to_z, lambda p: out3.at[layer, mats, p], lambda p: in3.at[layer, p, mats]
            )

        def start(self):
            self.core.start()

        def after_core(self):
            layer = self.layer
            self.core.wait()

            def add(i, carry):
                a, b = i // ny, i % ny
                out2[layer, a, b] = (
                    wt[layer, a, b, :, c].astype(F32) + in1[layer, a, b].astype(F32)
                ).astype(BF16)
                return carry

            lax.fori_loop(self.low * ny, self.high * ny, add, 0)
            self.ys.start()

        def after_y(self):
            layer = self.layer
            self.ys.finish()

            def add(a, carry):
                whole = out2[layer, a, y].astype(F32)
                for s in range(1, ny):
                    whole = whole + in2[layer, lax.rem(y + s, ny), a].astype(F32)
                out3[layer, a] = whole.astype(BF16)
                return carry

            lax.fori_loop(self.low, self.high, add, 0)
            self.zs.start()

        def after_z(self):
            layer = self.layer
            self.zs.finish()
            outs = (value_out, gate_out, project_out)
            for a, out in list(enumerate(outs))[self.low : self.high]:
                whole = out3[layer, a, z].astype(F32)
                for s in range(1, nz):
                    whole = whole + in3[layer, lax.rem(z + s, nz), a].astype(F32)
                out[layer] = whole

    class CrossScatter:
        def __init__(self, mat):
            self.mat = mat
            other = lax.rem(c + 1, nc)
            base = take(1)
            self.core = remote(
                wt.at[0, mat, :, :, other], in1.at[0, mat], base, base, to_c(other)
            )
            self.zs = Exchange(
                nz, z, to_z, lambda p: out2.at[0, mat, :, p], lambda p: in2z.at[p]
            )
            self.ys = Exchange(ny, y, to_y, lambda p: out3z.at[p], lambda p: in3z.at[p])

        def start(self):
            self.core.start()

        def after_core(self):
            self.core.wait()

            def add(b, carry):
                out2[0, self.mat, b] = (
                    wt[0, self.mat, b, :, c].astype(F32) + in1[0, self.mat, b].astype(F32)
                ).astype(BF16)
                return carry

            lax.fori_loop(0, ny, add, 0)
            self.zs.start()

        def after_z(self):
            self.zs.finish()

            def add(b, carry):
                whole = out2[0, self.mat, b, z].astype(F32)
                for s in range(1, nz):
                    whole = whole + in2z[lax.rem(z + s, nz), b].astype(F32)
                out3z[b] = whole.astype(BF16)
                return carry

            lax.fori_loop(0, ny, add, 0)
            self.ys.start()

        def after_y(self):
            self.ys.finish()
            whole = out3z[y].astype(F32)
            for s in range(1, ny):
                whole = whole + in3z[lax.rem(y + s, ny)].astype(F32)
            gate_out[0] = whole

    def weight_term(left, right, put):
        def step(i, carry):
            cols = pl.ds(pl.multiple_of(i * (depth // ny), depth // ny), depth // ny)
            whole = lax.dot_general(
                left[:, cols], right, (((0,), (0,)), ((), ())), preferred_element_type=F32
            )
            put(i, whole.astype(BF16))
            return carry

        lax.fori_loop(0, ny, step, 0)

    class TapSum:
        def __init__(self, layer):
            self.layer = layer
            self.one = Exchange(
                ny * nc, yc, to_yc, lambda p: tap1.at[layer, yc], lambda p: tap1.at[layer, p]
            )
            self.two = Exchange(
                nz, z, to_z, lambda p: tap2.at[layer, z], lambda p: tap2.at[layer, p]
            )

        def start(self):
            tap1[self.layer, yc] = tapsum[...].astype(BF16)
            self.one.start()

        def middle(self):
            self.one.finish()
            whole = tap1[self.layer, 0].astype(F32)
            for i in range(1, ny * nc):
                whole = whole + tap1[self.layer, i].astype(F32)
            tap2[self.layer, z] = whole.astype(BF16)
            self.two.start()

        def finish(self):
            self.two.finish()
            whole = tap2[self.layer, 0].astype(F32)
            for i in range(1, nz):
                whole = whole + tap2[self.layer, i].astype(F32)
            for h in range(2):
                tap_out[:, self.layer, halves(h)] = whole[h, 0:TAPS]

    def pair(group, step):
        lax.fori_loop(0, 2, lambda k, carry: step((2 * k + group) * CHUNK) or carry, 0)

    def tiles(first_row):
        return pl.ds(first_row // 8, CHUNK // 8)

    def rows_in(ref, first_row):
        return ref[tiles(first_row)].reshape(CHUNK, depth)

    def fill(src, dst):
        def step(t, carry):
            for q in range(STREAMS):
                dst[t, 2 * q : 2 * q + 2, :] = src[q, t].astype(F32)
            return carry

        lax.fori_loop(0, SEG, step, 0)

    def normalize(layer, rows_at, first_row):
        at = pl.ds(pl.multiple_of(first_row, CHUNK), CHUNK)
        rows = rows_at(first_row)
        centered = rows - jnp.mean(rows, axis=1, keepdims=True)
        scale = lax.rsqrt(jnp.mean(centered * centered, axis=1, keepdims=True) + EPSILON)
        out = centered * scale
        normed[layer, at] = out
        lnscale[layer, at] = jnp.broadcast_to(scale, (CHUNK, LANES))
        gath[layer, rows_of(x, first_row, CHUNK)] = out.astype(BF16)

    def back_rows(layer, summed, first_row):
        at = pl.ds(pl.multiple_of(first_row, CHUNK), CHUNK)
        grad = summed.rows(first_row)
        unit = normed[layer, at]
        cross = jnp.mean(grad * unit, axis=1, keepdims=True)
        scale = lnscale[layer, at][:, 0:1]
        return scale * (grad - jnp.mean(grad, axis=1, keepdims=True) - unit * cross)

    def forward(layer, gather, after, later):
        def block(s):
            rows = gath[layer, rows_of(s)]
            value = jnp.dot(rows, vw[layer], preferred_element_type=F32)
            gate = sigmoid(jnp.dot(rows, gw[layer], preferred_element_type=F32))
            for h in range(2):
                v, g = value[:, halves(h)], gate[:, halves(h)]
                keep = g * val[s]
                fv[layer, h, s] = keep
                fg[layer, h, s] = v * (1.0 - g) * keep
                low = (v * keep).astype(BF16)
                glu[rows_of(s), halves(h)] = low
                wide[layer, h, s + 1, MAIN : MAIN + ROWS] = low.astype(F32)

        gather.onward(0)
        gather.onward(2)
        block(x)
        gather.onward(1)
        gather.onward(3)
        after()
        gather.wait_left()
        block(left)
        gather.wait_right()
        block(right)
        gather.wait_far()
        block(far)
        edge = Halo(layer, glu, halo)
        edge.start()

        def conv(s, carry):
            widen(layer, s + 1)
            sums = []
            for h in range(2):
                mixed = convolve(layer, layer, h, s + 1, True)
                scaled[layer, h, s] = mixed
                sums.append(carry[h] + fold(mixed * val[s]))
            return tuple(sums)

        zero = jnp.zeros((8, LANES), F32)
        sums = lax.fori_loop(1, tp - 1, conv, (zero, zero))
        edge.wait()
        for h in range(2):
            wide[layer, h, 0, MAIN : MAIN + ROWS] = halo[layer, 0, :, halves(h)].astype(F32) * has_low
            wide[layer, h, tp + 1, MAIN : MAIN + ROWS] = (
                halo[layer, 1, :, halves(h)].astype(F32) * has_high
            )
        sums = lax.fori_loop(0, 2, lambda i, carry: conv(i * (tp - 1), carry), sums)
        sums = [jnp.sum(v, axis=0, keepdims=True) for v in sums]
        means = [v / jnp.maximum(local_count, 1.0) for v in sums]

        def spread(s, carry):
            out = []
            for h in range(2):
                gap = (scaled[layer, h, s] - means[h]) * val[s]
                out.append(carry[h] + fold(gap * gap))
            return tuple(out)

        squares = lax.fori_loop(0, tp, spread, (zero, zero))
        squares = [jnp.sum(v, axis=0, keepdims=True) for v in squares]
        count = jnp.zeros((1, LANES), F32) + local_count
        whole = reduce_tile(layer, sums + squares + [count], merge_moments, gather.sent, later)
        mean = [whole[h : h + 1] / total for h in range(2)]
        scale = [lax.rsqrt(whole[2 + h : 3 + h] / total + EPSILON) for h in range(2)]

        def activate(s):
            for h in range(2):
                unit = (scaled[layer, h, s] - mean[h]) * scale[h]
                shifted = gain[layer : layer + 1, halves(h)] * unit + shift[layer : layer + 1, halves(h)]
                sig = sigmoid(shifted)
                keep = sig * val[s]
                scaled[layer, h, s] = unit
                ds[layer, h, s] = keep * (1.0 + shifted * (1.0 - sig))
                act[layer, rows_of(s), halves(h)] = (shifted * keep).astype(BF16)

        return activate, scale

    def backward(layer, u, up_block, chan_scale, activate, meanwhile, between, weights_first):
        zero = jnp.zeros((8, LANES), F32)

        def one_block(s, carry):
            if activate is not None:
                activate(s)
            grad = lax.dot_general(
                ups[layer, rows_of(s)], pw[layer], (((1,), (1,)), ((), ())), preferred_element_type=F32
            )
            sums = list(carry)
            for h in range(2):
                g = grad[:, halves(h)] * ds[layer, h, s]
                unit = scaled[layer, h, s]
                ds[layer, h, s] = g
                lows[rows_of(s), halves(h)] = g.astype(BF16)
                lows[rows_of(s), halves(2 + h)] = unit.astype(BF16)
                sums[h] = sums[h] + fold(g)
                sums[2 + h] = sums[2 + h] + fold(g * unit)
            return tuple(sums)

        sums = up_block(one_block, (zero,) * 4)
        edge = Halo(layer, lows, halo2)
        edge.start()
        sums = [jnp.sum(v, axis=0, keepdims=True) for v in sums]

        if weights_first:
            scatters = [Scatter(layer, 2, 3), Scatter(layer, 0, 1), CrossScatter(1)]
        else:
            scatters = [Scatter(layer, 0, 3)]

        def project():
            def put(i, block):
                wt[layer, 2, i] = block.reshape(wt.shape[3:])

            weight_term(ups.at[layer], act[layer], put)
            if weights_first:
                scatters[0].start()

        whole = reduce_tile(2 + layer, sums, merge_sum, project)
        meanwhile()
        if weights_first:
            scatters[0].after_core()
        edge.wait()
        factor = [gain[layer : layer + 1, halves(h)] * chan_scale[h] for h in range(2)]
        first_mean = [whole[h : h + 1] / total for h in range(2)]
        cross_mean = [whole[2 + h : 3 + h] / total for h in range(2)]

        def mixed_grad(h, grad, unit, keep):
            return factor[h] * (grad - first_mean[h] - unit * cross_mean[h]) * keep

        def mix(s, carry):
            for h in range(2):
                wide[2, h, s + 1, MAIN : MAIN + ROWS] = mixed_grad(
                    h, ds[layer, h, s], scaled[layer, h, s], val[s]
                )
            return carry

        lax.fori_loop(0, tp, mix, 0)
        for side, has in enumerate((has_low, has_high)):
            for h in range(2):
                wide[2, h, side * (tp + 1), MAIN : MAIN + ROWS] = mixed_grad(
                    h,
                    halo2[layer, side, :, halves(h)].astype(F32),
                    halo2[layer, side, :, halves(2 + h)].astype(F32),
                    val[tp + side] * has,
                )

        def tap_terms():
            block = 8
            for h in range(2):

                def tap(i, sums):
                    s, t = i // (SEG // block), i % (SEG // block) * block
                    sums = list(sums)
                    grads = [
                        wide[2, h, s + 1, pl.ds(pl.multiple_of(MAIN + (t + k) * 8, 8), 8)]
                        for k in range(block)
                    ]
                    for k in range(block + TAPS - 1):
                        row = wide[layer, h, s + 1, pl.ds(pl.multiple_of((t + k) * 8, 8), 8)]
                        for m in range(block):
                            if 0 <= k - m < TAPS:
                                sums[k - m] = sums[k - m] + row * grads[m]
                    return tuple(sums)

                sums = lax.fori_loop(0, tp * SEG // block, tap, (zero,) * TAPS)
                for j in range(TAPS):
                    tapsum[h, j : j + 1, :] = jnp.sum(sums[j], axis=0, keepdims=True)
            total_taps = TapSum(layer)
            total_taps.start()
            return total_taps

        send = ScatterX(u)

        def lows_block(s):
            widen(2, s + 1)
            for h in range(2):
                grad = convolve(2, layer, h, s + 1, False)
                lows[rows_of(s), halves(h)] = (grad * fv[layer, h, s]).astype(BF16)
                lows[rows_of(s), slice(columns + h * LANES, columns + (h + 1) * LANES)] = (
                    grad * fg[layer, h, s]
                ).astype(BF16)

        def grad_block(s):
            whole = lax.dot_general(
                lows[rows_of(s), 0:columns],
                vw[layer],
                (((1,), (1,)), ((), ())),
                preferred_element_type=F32,
            ) + lax.dot_general(
                lows[rows_of(s), columns : 2 * columns],
                gw[layer],
                (((1,), (1,)), ((), ())),
                preferred_element_type=F32,
            )
            part[rows_of(s)] = whole.astype(BF16)

        def weights():
            if weights_first:
                for m in range(2):

                    def put_one(i, block):
                        wt[layer, m, i] = block.reshape(wt.shape[3:])

                    weight_term(gath.at[layer], lows[:, m * columns : (m + 1) * columns], put_one)
                    scatters[1 + m].start()
                    if m == 1:
                        scatters[1].after_core()
            else:

                def put(i, block):
                    wt[layer, 0, i] = block[:, 0:columns].reshape(wt.shape[3:])
                    wt[layer, 1, i] = block[:, columns:].reshape(wt.shape[3:])

                weight_term(gath.at[layer], lows[...], put)
                scatters[0].start()

        def block(s):
            if not weights_first:
                lows_block(s)
            grad_block(s)

        if weights_first:
            lax.fori_loop(0, tp, lambda s, carry: lows_block(s) or carry, 0)
            weights()
        block(far)
        send.send_far()
        if weights_first:
            scatters[2].after_core()
        block(right)
        block(left)
        send.send_early()
        between()
        block(x)
        send.combine_first()
        send.combine_last()
        if not weights_first:
            weights()
        return send, scatters, tap_terms

    tapsum[...] = jnp.zeros(tapsum.shape, F32)
    fill(frames, hid)
    gather = GatherX(gath, 0)
    for group in (0, 1):
        pair(group, lambda first_row: normalize(0, lambda r: rows_in(hid, r), first_row))
    pl.semaphore_wait(barrier, len(peers))
    for i in (0, 2, 1, 3):
        gather.push(i)
    fill(og, up)
    gather_up = GatherX(ups, 1)

    def copy_up(first_row):
        ups[1, rows_of(x, first_row, CHUNK)] = rows_in(up, first_row).astype(BF16)

    for group in (0, 1):
        pair(group, copy_up)
    for load in loads:
        load.wait()

    def send_up():
        for i in (0, 2, 1, 3):
            gather_up.push(i)

    def up_onward():
        for i in (0, 2, 1, 3):
            gather_up.onward(i)

    activate, scale0 = forward(0, gather, send_up, up_onward)
    branch = ScatterX(0)

    def project_block(s):
        activate(s)
        part[rows_of(s)] = jnp.dot(
            act[0, rows_of(s)], pw[0], preferred_element_type=F32
        ).astype(BF16)

    project_block(far)
    branch.send_far()
    project_block(right)
    project_block(left)
    branch.send_early()
    project_block(x)
    branch.combine_first()
    branch.combine_last()

    def hidden(first_row):
        return (rows_in(hid, first_row) + branch.rows(first_row)).astype(BF16).astype(F32)

    gather = GatherX(gath, 1)
    for group in (0, 1):
        branch.landed(group)
        branch.landed(group + 2)
        pair(group, lambda first_row: normalize(1, hidden, first_row))
        gather.push(group)
        gather.push(group + 2)
    branch.sent()

    def nothing():
        return None

    activate, scale1 = forward(1, gather, nothing, None)
    gather_up.wait_left()
    gather_up.wait_right()
    gather_up.wait_far()
    gather_up.sent()

    def all_blocks(block, carry):
        return lax.fori_loop(0, tp, block, carry)

    send, (scatter1,), tap_terms1 = backward(
        1, 1, all_blocks, scale1, activate, nothing, nothing, False
    )
    gather0 = GatherX(ups, 0)

    def next_up(first_row):
        whole = rows_in(up, first_row) + back_rows(1, send, first_row)
        up[tiles(first_row)] = whole.reshape(CHUNK // 8, 8, depth)
        ups[0, rows_of(x, first_row, CHUNK)] = whole.astype(BF16)

    for group in (0, 1):
        send.landed(group)
        send.landed(group + 2)
        pair(group, next_up)
        gather0.push(group)
        gather0.push(group + 2)
        if group == 0:
            scatter1.after_core()
    taps1 = []

    def in_turn(block, carry):
        gather0.onward(0)
        gather0.onward(2)
        carry = block(x, carry)
        gather0.onward(1)
        gather0.onward(3)
        send.sent()
        taps1.append(tap_terms1())
        gather0.wait_left()
        carry = block(left, carry)
        gather0.wait_right()
        carry = block(right, carry)
        gather0.wait_far()
        carry = block(far, carry)
        gather0.sent()
        return carry

    last, scatters0, tap_terms0 = backward(
        0, 2, in_turn, scale0, None, lambda: taps1[0].middle(), scatter1.after_y, True
    )
    taps0 = tap_terms0()
    scatters0[0].after_y()

    def last_up(first_row):
        whole = rows_in(up, first_row) + back_rows(0, last, first_row)
        up[tiles(first_row)] = whole.reshape(CHUNK // 8, 8, depth)

        def put(i, carry):
            t = first_row // 8 + i
            for q in range(STREAMS):
                up_out[q, t] = up[t, 2 * q : 2 * q + 2, :]
            return carry

        lax.fori_loop(0, CHUNK // 8, put, 0)

    scatters0[1].after_y()
    last.landed(0)
    last.landed(2)
    pair(0, last_up)
    taps0.middle()
    scatters0[2].after_z()
    last.landed(1)
    last.landed(3)
    pair(1, last_up)
    last.sent()
    taps1[0].finish()
    scatter1.after_z()
    scatters0[0].after_z()
    scatters0[1].after_z()
    scatters0[2].after_y()
    taps0.finish()


def scratch(ctx, tp, layers, depth, columns):
    ny, nz, nc = grid_of(ctx)
    rows = tp * ROWS
    piece = depth // ctx
    return [
        pltpu.VMEM((layers, depth, columns), BF16),
        pltpu.VMEM((layers, depth, columns), BF16),
        pltpu.VMEM((layers, columns, depth), BF16),
        pltpu.VMEM((SEG, 8, depth), F32),
        pltpu.VMEM((SEG, 8, depth), F32),
        pltpu.VMEM((tp + 2, ROWS, LANES), F32),
        pltpu.VMEM((layers, rows, depth), BF16),
        pltpu.VMEM((layers, rows, depth), BF16),
        pltpu.VMEM((rows, depth), BF16),
        pltpu.VMEM((3, ROWS, depth), BF16),
        pltpu.VMEM((3, 2, ROWS, depth), BF16),
        pltpu.VMEM((layers, ROWS, depth), F32),
        pltpu.VMEM((layers, ROWS, LANES), F32),
        pltpu.VMEM((layers, 2, tp, ROWS, LANES), F32),
        pltpu.VMEM((layers, 2, tp, ROWS, LANES), F32),
        pltpu.VMEM((layers, 2, tp, ROWS, LANES), F32),
        pltpu.VMEM((layers, 2, tp, ROWS, LANES), F32),
        pltpu.VMEM((layers, rows, columns), BF16),
        pltpu.VMEM((rows, columns), BF16),
        pltpu.VMEM((3, 2, tp + 2, WIDE, LANES), F32),
        pltpu.VMEM((rows, 2 * columns), BF16),
        pltpu.VMEM((layers, 2, ROWS, columns), BF16),
        pltpu.VMEM((layers, 2, ROWS, 2 * columns), BF16),
        pltpu.VMEM((4, ny * nc, 8, LANES), F32),
        pltpu.VMEM((4, nz, 8, LANES), F32),
        pltpu.VMEM((2, TAPS + 1, LANES), F32),
        pltpu.VMEM((layers, ny * nc, 2, TAPS + 1, LANES), BF16),
        pltpu.VMEM((layers, nz, 2, TAPS + 1, LANES), BF16),
        pltpu.VMEM((layers, 3, ny, nz, nc, piece, columns), BF16),
        pltpu.VMEM((layers, 3, ny, nz, piece, columns), BF16),
        pltpu.VMEM((layers, 3, ny, nz, piece, columns), BF16),
        pltpu.VMEM((layers, ny, 3, nz, piece, columns), BF16),
        pltpu.VMEM((layers, 3, nz, piece, columns), BF16),
        pltpu.VMEM((layers, nz, 3, piece, columns), BF16),
        pltpu.VMEM((nz, ny, piece, columns), BF16),
        pltpu.VMEM((ny, piece, columns), BF16),
        pltpu.VMEM((ny, piece, columns), BF16),
        pltpu.SemaphoreType.DMA((3,)),
        pltpu.SemaphoreType.DMA((256,)),
        pltpu.SemaphoreType.DMA((256,)),
    ]


def flush(*refs):
    count = len(refs) // 2
    for i in range(count):
        refs[count + i][...] = refs[i][...]


def on_device(
    frames,
    lengths,
    value_weight,
    gate_weight,
    tap_weights,
    norm_gain,
    norm_shift,
    project_weight,
    output_grad,
):
    ctx, tp = lax.axis_size("ctx"), lax.axis_size("tp")
    layers, depth, columns = value_weight.shape
    piece = depth // ctx
    vmem = pl.BlockSpec(memory_space=pltpu.VMEM)
    smem = pl.BlockSpec(memory_space=pltpu.SMEM)
    hbm = pl.BlockSpec(memory_space=pl.ANY)
    recs = frames.shape[1]
    split = (STREAMS, SEG, recs, depth)
    shapes = (
        jax.ShapeDtypeStruct(split, F32),
        jax.ShapeDtypeStruct((layers, piece, columns), F32),
        jax.ShapeDtypeStruct((layers, piece, columns), F32),
        jax.ShapeDtypeStruct((layers, piece, columns), F32),
        jax.ShapeDtypeStruct((TAPS, layers, columns), F32),
    )
    results = pl.pallas_call(
        functools.partial(fused, ctx, tp),
        out_shape=shapes,
        in_specs=[vmem, vmem, smem, hbm, hbm, hbm, vmem, vmem, vmem],
        out_specs=(vmem,) * 5,
        scratch_shapes=scratch(ctx, tp, layers, depth, columns),
        compiler_params=pltpu.CompilerParams(
            collective_id=0, has_side_effects=True, vmem_limit_bytes=60 * 1024 * 1024
        ),
    )(
        frames.reshape(split),
        output_grad.reshape(split),
        lengths,
        value_weight,
        gate_weight,
        project_weight,
        jnp.swapaxes(tap_weights, 0, 1),
        norm_gain,
        norm_shift,
    )
    up, value, gate, project, tap = pl.pallas_call(
        flush,
        out_shape=shapes,
        in_specs=[vmem] * 5,
        out_specs=(vmem,) * 5,
    )(*results)
    return (
        up.reshape(frames.shape),
        value,
        gate,
        jnp.swapaxes(project, 1, 2),
        jnp.swapaxes(tap, 0, 1),
    )


def solution(mesh):
    in_specs = (
        P(("ctx", "tp"), None, None),
        P(),
        P(None, None, "tp"),
        P(None, None, "tp"),
        P(None, None, "tp"),
        P(None, "tp"),
        P(None, "tp"),
        P(None, "tp", None),
        P(("ctx", "tp"), None, None),
    )
    out_specs = (
        P(("ctx", "tp"), None, None),
        P(None, "ctx", "tp"),
        P(None, "ctx", "tp"),
        P(None, "tp", "ctx"),
        P(None, None, "tp"),
    )
    return jax.shard_map(
        on_device, mesh=mesh, in_specs=in_specs, out_specs=out_specs, check_vma=False
    )
```

```python
import functools

import jax
import jax.numpy as jnp
from jax import lax
from jax.experimental import pallas as pl
from jax.experimental.pallas import tpu as pltpu
from jax.sharding import PartitionSpec as P

EPSILON = 1e-05
MESH = pl.DeviceIdType.MESH
F32, BF16 = jnp.float32, jnp.bfloat16
TAPS, REACH = 31, 15
CHUNK = 32
LANES = 128
STREAMS, SEG = 4, 16
ROWS = SEG * 8
MAIN = REACH * 8
WIDE = (SEG + 2 * REACH) * 8


def grid_of(ctx):
    return {64: (4, 8, 2), 8: (2, 2, 2)}[ctx]


def rows_of(slot, first=0, count=ROWS):
    return pl.ds(pl.multiple_of(slot * ROWS + first, 16), count)


def sigmoid(v):
    return 1.0 / (1.0 + jnp.exp(-v))


def fused(
    ctx,
    tp,
    frames_in,
    og_in,
    lengths,
    vw_in,
    gw_in,
    pw_in,
    taps_in,
    gain_in,
    shift_in,
    up,
    value_out,
    gate_out,
    project_out,
    tap_out,
    vw,
    gw,
    pw,
    frames,
    og,
    taps,
    gain,
    shift,
    hid,
    val,
    gath,
    ups,
    part,
    farland,
    land,
    normed,
    lnscale,
    fv,
    fg,
    scaled,
    ds,
    act,
    glu,
    wide,
    lows,
    halo,
    halo2,
    first,
    second,
    tapsum,
    tap1,
    tap2,
    wt,
    in1,
    out2,
    in2,
    out3,
    in3,
    early,
    in2z,
    out3z,
    in3z,
    lsem,
    ssem,
    rsem,
):
    ny, nz, nc = grid_of(ctx)
    pos = lax.axis_index("ctx")
    x = lax.axis_index("tp")
    y, z, c = pos // (nz * nc), (pos // nc) % nz, pos % nc
    depth = gath.shape[2]
    columns = value_out.shape[2]

    def to_x(p):
        return {"tp": p}

    def to_yc(p):
        return {"ctx": ((p // nc) * nz + z) * nc + p % nc}

    def to_y(p):
        return {"ctx": (p * nz + z) * nc + c}

    def to_z(p):
        return {"ctx": (y * nz + p) * nc + c}

    def to_c(p):
        return {"ctx": (y * nz + z) * nc + p}

    yc = y * nc + c
    following = {"ctx": lax.rem(pos + 1, ctx)}
    previous = {"ctx": lax.rem(pos + ctx - 1, ctx)}

    loads = [
        pltpu.make_async_copy(src, dst, lsem.at[i])
        for i, (src, dst) in enumerate(
            (
                (frames_in, frames),
                (og_in, og),
                (vw_in, vw),
                (gw_in, gw),
                (taps_in, taps),
                (gain_in, gain),
                (shift_in, shift),
                (pw_in, pw),
            )
        )
    ]
    for load in loads:
        load.start()

    barrier = pltpu.get_barrier_semaphore()
    peers = [to_x(lax.rem(x + s, tp)) for s in range(1, tp)]
    peers += [to_yc(lax.rem(yc + s, ny * nc)) for s in range(1, ny * nc)]
    peers += [to_z(lax.rem(z + s, nz)) for s in range(1, nz)]
    peers += [following, previous]
    for peer in peers:
        pl.semaphore_signal(barrier, inc=1, device_id=peer, device_id_type=MESH)
    taken = [0]

    def take(n):
        taken[0] += n
        return taken[0] - n

    def remote(src, dst, send, recv, target):
        return pltpu.make_async_remote_copy(
            src_ref=src,
            dst_ref=dst,
            send_sem=ssem.at[send],
            recv_sem=rsem.at[recv],
            device_id=target,
            device_id_type=MESH,
        )

    class Exchange:
        def __init__(self, count, me, target, src, dst):
            self.count, self.me, self.target, self.src, self.dst = count, me, target, src, dst
            self.base = take(count)
            self.order = list(range(1, count))

        def peer(self, step):
            return lax.rem(self.me + step, self.count)

        def send(self, step):
            p = self.peer(step)
            remote(
                self.src(p), self.dst(self.me), self.base + step, self.base + self.me, self.target(p)
            ).start()

        def start(self):
            for step in self.order:
                self.send(step)

        def landed(self, step):
            p = self.peer(step)
            remote(
                self.src(p), self.dst(p), self.base + step, self.base + p, self.target(p)
            ).wait_recv()

        def sent(self):
            for step in self.order:
                p = self.peer(step)
                remote(
                    self.src(p), self.dst(self.me), self.base + step, self.base + self.me, self.target(p)
                ).wait_send()

        def finish(self):
            for step in self.order:
                self.landed(step)
            self.sent()

    right, left, far = lax.rem(x + 1, tp), lax.rem(x + 3, tp), lax.rem(x + 2, tp)

    class GatherX:
        def __init__(self, buf, which):
            self.rows = lambda d, i: buf.at[which, rows_of(d, i * CHUNK, CHUNK)]
            self.base = take(12)

        def copy(self, owner, i, sem, target):
            ref = self.rows(owner, i)
            return remote(ref, ref, self.base + sem, self.base + sem, to_x(target))

        def push(self, i):
            self.copy(x, i, i, right).start()
            self.copy(x, i, 4 + i, left).start()

        def onward(self, i):
            if i < 2:
                self.copy(left, i, i, right).wait_recv()
                self.copy(left, i, 8 + i, right).start()
            else:
                self.copy(right, i, 4 + i, left).wait_recv()
                self.copy(right, i, 8 + i, left).start()

        def wait_left(self):
            for i in (2, 3):
                self.copy(left, i, i, right).wait_recv()

        def wait_right(self):
            for i in (0, 1):
                self.copy(right, i, 4 + i, left).wait_recv()

        def wait_far(self):
            for i in (0, 2, 1, 3):
                self.copy(far, i, 8 + i, right).wait_recv()

        def sent(self):
            for i in range(4):
                self.copy(x, i, i, right).wait_send()
                self.copy(x, i, 4 + i, left).wait_send()
                if i < 2:
                    self.copy(left, i, 8 + i, right).wait_send()
                else:
                    self.copy(right, i, 8 + i, left).wait_send()

    class ScatterX:
        def __init__(self, u):
            self.u = u
            self.base = take(12)

        def far_copy(self, i):
            return remote(
                part.at[rows_of(far, i * CHUNK, CHUNK)],
                farland.at[self.u, pl.ds(i * CHUNK, CHUNK)],
                self.base + i,
                self.base + i,
                to_x(right if i < 2 else left),
            )

        def near_copy(self, way, i):
            sem = self.base + 4 + 4 * way + i
            return remote(
                part.at[rows_of(left if way else right, i * CHUNK, CHUNK)],
                land.at[self.u, way, pl.ds(i * CHUNK, CHUNK)],
                sem,
                sem,
                to_x(left if way else right),
            )

        def send_far(self):
            for i in (0, 2, 1, 3):
                self.far_copy(i).start()

        def send_early(self):
            self.near_copy(0, 2).start()
            self.near_copy(1, 0).start()

        def send_late(self):
            self.near_copy(0, 3).start()
            self.near_copy(1, 1).start()

        def combine(self, i):
            self.far_copy(i).wait_recv()
            way = 0 if i < 2 else 1
            at = rows_of(left if way else right, i * CHUNK, CHUNK)
            part[at] = (
                part[at].astype(F32) + farland[self.u, i * CHUNK : (i + 1) * CHUNK].astype(F32)
            ).astype(BF16)
            self.near_copy(way, i).start()

        def combine_first(self):
            self.combine(0)
            self.combine(2)

        def combine_last(self):
            self.send_late()
            self.combine(1)
            self.combine(3)

        def landed(self, i):
            self.near_copy(0, i).wait_recv()
            self.near_copy(1, i).wait_recv()

        def sent(self):
            for i in range(4):
                self.far_copy(i).wait_send()
                self.near_copy(0, i).wait_send()
                self.near_copy(1, i).wait_send()

        def rows(self, first_row):
            at = pl.ds(pl.multiple_of(first_row, CHUNK), CHUNK)
            return (
                part[rows_of(x, first_row, CHUNK)].astype(F32)
                + land[self.u, 0, at].astype(F32)
                + land[self.u, 1, at].astype(F32)
            )

    len0, len1 = lengths[0], lengths[1]
    start_frame = pos * (tp * STREAMS * SEG)
    t_in = lax.broadcasted_iota(jnp.int32, (SEG, 8, LANES), 0)
    sub = lax.broadcasted_iota(jnp.int32, (SEG, 8, LANES), 1)
    limit = jnp.where(sub % 2 == 0, len0, len1)
    for s in range(-1, tp + 1):
        frame = start_frame + s * (STREAMS * SEG) + (sub // 2) * SEG + t_in
        val[tp + 1 if s == tp else s if s >= 0 else tp] = jnp.where(frame < limit, 1.0, 0.0).astype(F32).reshape(ROWS, LANES)
    span = tp * STREAMS * SEG
    total = (len0 + len1).astype(F32)
    local_count = (
        jnp.clip(len0 - start_frame, 0, span) + jnp.clip(len1 - start_frame, 0, span)
    ).astype(F32)

    def halves(h):
        return slice(h * LANES, (h + 1) * LANES)

    def reduce_tile(u, rows, merge, meanwhile=None, later=None):
        first[u, yc] = jnp.zeros((8, LANES), F32)
        for i, row in enumerate(rows):
            first[u, yc, i : i + 1, :] = row
        one = Exchange(
            ny * nc, yc, to_yc, lambda p: first.at[u, yc], lambda p: first.at[u, p]
        )
        one.start()
        if meanwhile is not None:
            meanwhile()
        one.finish()
        second[u, z] = merge([first[u, i] for i in range(ny * nc)])
        two = Exchange(nz, z, to_z, lambda p: second.at[u, z], lambda p: second.at[u, p])
        two.start()
        if later is not None:
            later()
        two.finish()
        return merge([second[u, i] for i in range(nz)])

    def merge_sum(tiles):
        whole = tiles[0]
        for tile in tiles[1:]:
            whole = whole + tile
        return whole

    def merge_moments(tiles):
        whole = merge_sum(tiles)
        mean = whole[0:2] / jnp.maximum(whole[4:5], 1.0)
        square = whole[2:4]
        for tile in tiles:
            gap = tile[0:2] / jnp.maximum(tile[4:5], 1.0) - mean
            square = square + tile[4:5] * gap * gap
        return jnp.concatenate([whole[0:2], square, whole[4:8]], axis=0)

    def fold(v):
        return jnp.sum(v.reshape(SEG, 8, LANES), axis=0)

    tile_sub = lax.broadcasted_iota(jnp.int32, (REACH, 8, LANES), 1)

    def widen(e, s):
        for h in range(2):
            cur = wide[e, h, s, MAIN + 8 : MAIN + ROWS].reshape(REACH, 8, LANES)
            old = wide[e, h, s - 1, MAIN + 8 : MAIN + ROWS].reshape(REACH, 8, LANES)
            low = jnp.where(tile_sub < 2, pltpu.roll(old, 2, 1), pltpu.roll(cur, 2, 1))
            wide[e, h, s, 0:MAIN] = low.reshape(MAIN, LANES)
            cur = wide[e, h, s, MAIN : MAIN + ROWS - 8].reshape(REACH, 8, LANES)
            new = wide[e, h, s + 1, MAIN : MAIN + ROWS - 8].reshape(REACH, 8, LANES)
            high = jnp.where(tile_sub >= 6, pltpu.roll(new, 6, 1), pltpu.roll(cur, 6, 1))
            wide[e, h, s, MAIN + ROWS : WIDE] = high.reshape(MAIN, LANES)

    def convolve(e, layer, h, s, forward):
        result = None
        for j in range(TAPS):
            at = (j if forward else TAPS - 1 - j) * 8
            term = taps[j, layer : layer + 1, halves(h)] * wide[e, h, s, at : at + ROWS]
            result = term if result is None else result + term
        return result

    class Halo:
        def __init__(self, u, src, dst):
            self.u = u
            base = take(2)
            self.up = remote(src.at[rows_of(tp - 1)], dst.at[u, 0], base, base, following)
            self.down = remote(src.at[rows_of(0)], dst.at[u, 1], base + 1, base + 1, previous)

        def start(self):
            self.up.start()
            self.down.start()

        def wait(self):
            self.up.wait()
            self.down.wait()

    has_low = (pos > 0).astype(F32)
    has_high = (pos < ctx - 1).astype(F32)

    class Scatter:
        def __init__(self, layer, low, high):
            self.layer, self.low, self.high = layer, low, high
            other = lax.rem(c + 1, nc)
            base = take(1)
            mats = slice(low, high)
            self.core = remote(
                wt.at[layer, mats, :, :, other], in1.at[layer, mats], base, base, to_c(other)
            )
            self.ys = Exchange(
                ny, y, to_y, lambda p: out2.at[layer, mats, p], lambda p: in2.at[layer, p, mats]
            )
            self.zs = Exchange(
                nz, z, to_z, lambda p: out3.at[layer, mats, p], lambda p: in3.at[layer, p, mats]
            )

        def start(self):
            self.core.start()

        def after_core(self):
            layer = self.layer
            self.core.wait()

            def add(i, carry):
                a, b = i // ny, i % ny
                out2[layer, a, b] = (
                    wt[layer, a, b, :, c].astype(F32) + in1[layer, a, b].astype(F32)
                ).astype(BF16)
                return carry

            lax.fori_loop(self.low * ny, self.high * ny, add, 0)
            self.ys.start()

        def after_y(self):
            layer = self.layer
            self.ys.finish()

            def add(a, carry):
                whole = out2[layer, a, y].astype(F32)
                for s in range(1, ny):
                    whole = whole + in2[layer, lax.rem(y + s, ny), a].astype(F32)
                out3[layer, a] = whole.astype(BF16)
                return carry

            lax.fori_loop(self.low, self.high, add, 0)
            self.zs.start()

        def after_z(self):
            layer = self.layer
            self.zs.finish()
            outs = (value_out, gate_out, project_out)
            for a, out in list(enumerate(outs))[self.low : self.high]:
                whole = out3[layer, a, z].astype(F32)
                for s in range(1, nz):
                    whole = whole + in3[layer, lax.rem(z + s, nz), a].astype(F32)
                out[layer] = whole

    class CrossScatter:
        def __init__(self, mat):
            self.mat = mat
            other = lax.rem(c + 1, nc)
            base = take(1)
            self.core = remote(
                wt.at[0, mat, :, :, other], in1.at[0, mat], base, base, to_c(other)
            )
            self.zs = Exchange(
                nz, z, to_z, lambda p: out2.at[0, mat, :, p], lambda p: in2z.at[p]
            )
            self.ys = Exchange(ny, y, to_y, lambda p: out3z.at[p], lambda p: in3z.at[p])

        def start(self):
            self.core.start()

        def after_core(self):
            self.core.wait()

            def add(b, carry):
                out2[0, self.mat, b] = (
                    wt[0, self.mat, b, :, c].astype(F32) + in1[0, self.mat, b].astype(F32)
                ).astype(BF16)
                return carry

            lax.fori_loop(0, ny, add, 0)
            self.zs.start()

        def after_z(self):
            self.zs.finish()

            def add(b, carry):
                whole = out2[0, self.mat, b, z].astype(F32)
                for s in range(1, nz):
                    whole = whole + in2z[lax.rem(z + s, nz), b].astype(F32)
                out3z[b] = whole.astype(BF16)
                return carry

            lax.fori_loop(0, ny, add, 0)
            self.ys.start()

        def after_y(self):
            self.ys.finish()
            whole = out3z[y].astype(F32)
            for s in range(1, ny):
                whole = whole + in3z[lax.rem(y + s, ny)].astype(F32)
            gate_out[0] = whole

    def weight_term(left, right, put):
        def step(i, carry):
            cols = pl.ds(pl.multiple_of(i * (depth // ny), depth // ny), depth // ny)
            whole = lax.dot_general(
                left[:, cols], right, (((0,), (0,)), ((), ())), preferred_element_type=F32
            )
            put(i, whole.astype(BF16))
            return carry

        lax.fori_loop(0, ny, step, 0)

    class TapSum:
        def __init__(self, layer):
            self.layer = layer
            self.one = Exchange(
                ny * nc, yc, to_yc, lambda p: tap1.at[layer, yc], lambda p: tap1.at[layer, p]
            )
            self.two = Exchange(
                nz, z, to_z, lambda p: tap2.at[layer, z], lambda p: tap2.at[layer, p]
            )

        def start(self):
            tap1[self.layer, yc] = tapsum[...].astype(BF16)
            self.one.start()

        def middle(self):
            self.one.finish()
            whole = tap1[self.layer, 0].astype(F32)
            for i in range(1, ny * nc):
                whole = whole + tap1[self.layer, i].astype(F32)
            tap2[self.layer, z] = whole.astype(BF16)
            self.two.start()

        def finish(self):
            self.two.finish()
            whole = tap2[self.layer, 0].astype(F32)
            for i in range(1, nz):
                whole = whole + tap2[self.layer, i].astype(F32)
            for h in range(2):
                tap_out[:, self.layer, halves(h)] = whole[h, 0:TAPS]

    def pair(group, step):
        lax.fori_loop(0, 2, lambda k, carry: step((2 * k + group) * CHUNK) or carry, 0)

    def tiles(first_row):
        return pl.ds(first_row // 8, CHUNK // 8)

    def rows_in(ref, first_row):
        return ref[tiles(first_row)].reshape(CHUNK, depth)

    def fill(src, dst):
        def step(t, carry):
            for q in range(STREAMS):
                dst[t, 2 * q : 2 * q + 2, :] = src[q, t].astype(F32)
            return carry

        lax.fori_loop(0, SEG, step, 0)

    def normalize(layer, rows_at, first_row):
        at = pl.ds(pl.multiple_of(first_row, CHUNK), CHUNK)
        rows = rows_at(first_row)
        centered = rows - jnp.mean(rows, axis=1, keepdims=True)
        scale = lax.rsqrt(jnp.mean(centered * centered, axis=1, keepdims=True) + EPSILON)
        out = centered * scale
        normed[layer, at] = out
        lnscale[layer, at] = jnp.broadcast_to(scale, (CHUNK, LANES))
        gath[layer, rows_of(x, first_row, CHUNK)] = out.astype(BF16)

    def back_rows(layer, summed, first_row):
        at = pl.ds(pl.multiple_of(first_row, CHUNK), CHUNK)
        grad = summed.rows(first_row)
        unit = normed[layer, at]
        cross = jnp.mean(grad * unit, axis=1, keepdims=True)
        scale = lnscale[layer, at][:, 0:1]
        return scale * (grad - jnp.mean(grad, axis=1, keepdims=True) - unit * cross)

    def forward(layer, gather, after, later):
        def block(s):
            rows = gath[layer, rows_of(s)]
            value = jnp.dot(rows, vw[layer], preferred_element_type=F32)
            gate = sigmoid(jnp.dot(rows, gw[layer], preferred_element_type=F32))
            for h in range(2):
                v, g = value[:, halves(h)], gate[:, halves(h)]
                keep = g * val[s]
                fv[layer, h, s] = keep
                fg[layer, h, s] = v * (1.0 - g) * keep
                low = (v * keep).astype(BF16)
                glu[rows_of(s), halves(h)] = low
                wide[layer, h, s + 1, MAIN : MAIN + ROWS] = low.astype(F32)

        gather.onward(0)
        gather.onward(2)
        block(x)
        gather.onward(1)
        gather.onward(3)
        after()
        gather.wait_left()
        block(left)
        gather.wait_right()
        block(right)
        gather.wait_far()
        block(far)
        edge = Halo(layer, glu, halo)
        edge.start()

        def conv(s, carry):
            widen(layer, s + 1)
            sums = []
            for h in range(2):
                mixed = convolve(layer, layer, h, s + 1, True)
                scaled[layer, h, s] = mixed
                sums.append(carry[h] + fold(mixed * val[s]))
            return tuple(sums)

        zero = jnp.zeros((8, LANES), F32)
        for h in range(2):
            for side in (0, tp + 1):
                wide[layer, h, side, MAIN : MAIN + ROWS] = jnp.zeros((ROWS, LANES), F32)
        sums = list(lax.fori_loop(0, tp, conv, (zero, zero)))
        edge.wait()
        for h in range(2):
            tap_rows = [taps[j, layer : layer + 1, halves(h)] for j in range(TAPS)]
            low = halo[layer, 0, :, halves(h)].astype(F32) * has_low
            high = halo[layer, 1, :, halves(h)].astype(F32) * has_high
            wide[layer, h, 0, MAIN : MAIN + ROWS] = low
            wide[layer, h, tp + 1, MAIN : MAIN + ROWS] = high
            low = low[8:].reshape(REACH, 8, LANES)
            high = high[: MAIN].reshape(REACH, 8, LANES)
            low = jnp.where(tile_sub < 2, pltpu.roll(low, 2, 1), 0.0)
            high = jnp.where(tile_sub >= 6, pltpu.roll(high, 6, 1), 0.0)
            wide[layer, h, 1, 0:MAIN] += low.reshape(MAIN, LANES)
            wide[layer, h, tp, MAIN + ROWS : WIDE] += high.reshape(MAIN, LANES)
            for t in range(REACH):
                at = slice(t * 8, t * 8 + 8)
                add = None
                for j in range(REACH - t):
                    term = tap_rows[j] * low[t + j]
                    add = term if add is None else add + term
                scaled[layer, h, 0, at] += add
                sums[h] = sums[h] + add * val[0, at]
            for t in range(1, SEG):
                at = slice(t * 8, t * 8 + 8)
                add = None
                for i in range(t):
                    term = tap_rows[SEG + REACH + i - t] * high[i]
                    add = term if add is None else add + term
                scaled[layer, h, tp - 1, at] += add
                sums[h] = sums[h] + add * val[tp - 1, at]
        sums = [jnp.sum(v, axis=0, keepdims=True) for v in sums]
        means = [v / jnp.maximum(local_count, 1.0) for v in sums]

        def spread(s, carry):
            out = []
            for h in range(2):
                gap = (scaled[layer, h, s] - means[h]) * val[s]
                out.append(carry[h] + fold(gap * gap))
            return tuple(out)

        squares = lax.fori_loop(0, tp, spread, (zero, zero))
        squares = [jnp.sum(v, axis=0, keepdims=True) for v in squares]
        count = jnp.zeros((1, LANES), F32) + local_count
        whole = reduce_tile(layer, sums + squares + [count], merge_moments, gather.sent, later)
        mean = [whole[h : h + 1] / total for h in range(2)]
        scale = [lax.rsqrt(whole[2 + h : 3 + h] / total + EPSILON) for h in range(2)]

        def activate(s):
            for h in range(2):
                unit = (scaled[layer, h, s] - mean[h]) * scale[h]
                shifted = gain[layer : layer + 1, halves(h)] * unit + shift[layer : layer + 1, halves(h)]
                sig = sigmoid(shifted)
                keep = sig * val[s]
                scaled[layer, h, s] = unit
                ds[layer, h, s] = keep * (1.0 + shifted * (1.0 - sig))
                act[layer, rows_of(s), halves(h)] = (shifted * keep).astype(BF16)

        return activate, scale

    def act_grad(layer, s):
        return lax.dot_general(
            ups[layer, rows_of(s)], pw[layer], (((1,), (1,)), ((), ())), preferred_element_type=F32
        )

    def backward(layer, u, up_block, chan_scale, activate, meanwhile, between, weights_first):
        zero = jnp.zeros((8, LANES), F32)

        def one_block(s, carry):
            if activate is not None:
                activate(s)
            grad = act_grad(layer, s) if activate is None else early[rows_of(s)]
            sums = list(carry)
            for h in range(2):
                g = grad[:, halves(h)] * ds[layer, h, s]
                unit = scaled[layer, h, s]
                ds[layer, h, s] = g
                lows[rows_of(s), halves(h)] = g.astype(BF16)
                lows[rows_of(s), halves(2 + h)] = unit.astype(BF16)
                sums[h] = sums[h] + fold(g)
                sums[2 + h] = sums[2 + h] + fold(g * unit)
            return tuple(sums)

        sums = up_block(one_block, (zero,) * 4)
        edge = Halo(layer, lows, halo2)
        edge.start()
        sums = [jnp.sum(v, axis=0, keepdims=True) for v in sums]

        if weights_first:
            scatters = [Scatter(layer, 2, 3), Scatter(layer, 0, 1), CrossScatter(1)]
        else:
            scatters = [Scatter(layer, 0, 3)]

        def project():
            def put(i, block):
                wt[layer, 2, i] = block.reshape(wt.shape[3:])

            weight_term(ups.at[layer], act[layer], put)
            if weights_first:
                scatters[0].start()

        whole = reduce_tile(2 + layer, sums, merge_sum, project)
        edge.wait()
        factor = [gain[layer : layer + 1, halves(h)] * chan_scale[h] for h in range(2)]
        first_mean = [whole[h : h + 1] / total for h in range(2)]
        cross_mean = [whole[2 + h : 3 + h] / total for h in range(2)]

        def mixed_grad(h, grad, unit, keep):
            return factor[h] * (grad - first_mean[h] - unit * cross_mean[h]) * keep

        def mix(s, carry):
            for h in range(2):
                wide[2, h, s + 1, MAIN : MAIN + ROWS] = mixed_grad(
                    h, ds[layer, h, s], scaled[layer, h, s], val[s]
                )
            return carry

        lax.fori_loop(0, tp, mix, 0)
        for side, has in enumerate((has_low, has_high)):
            for h in range(2):
                wide[2, h, side * (tp + 1), MAIN : MAIN + ROWS] = mixed_grad(
                    h,
                    halo2[layer, side, :, halves(h)].astype(F32),
                    halo2[layer, side, :, halves(2 + h)].astype(F32),
                    val[tp + side] * has,
                )

        def tap_terms():
            block = 8
            for h in range(2):

                def tap(i, sums):
                    s, t = i // (SEG // block), i % (SEG // block) * block
                    sums = list(sums)
                    grads = [
                        wide[2, h, s + 1, pl.ds(pl.multiple_of(MAIN + (t + k) * 8, 8), 8)]
                        for k in range(block)
                    ]
                    for k in range(block + TAPS - 1):
                        row = wide[layer, h, s + 1, pl.ds(pl.multiple_of((t + k) * 8, 8), 8)]
                        for m in range(block):
                            if 0 <= k - m < TAPS:
                                sums[k - m] = sums[k - m] + row * grads[m]
                    return tuple(sums)

                sums = lax.fori_loop(0, tp * SEG // block, tap, (zero,) * TAPS)
                for j in range(TAPS):
                    tapsum[h, j : j + 1, :] = jnp.sum(sums[j], axis=0, keepdims=True)
            total_taps = TapSum(layer)
            total_taps.start()
            return total_taps

        send = ScatterX(u)

        def lows_block(s):
            widen(2, s + 1)
            for h in range(2):
                grad = convolve(2, layer, h, s + 1, False)
                lows[rows_of(s), halves(h)] = (grad * fv[layer, h, s]).astype(BF16)
                lows[rows_of(s), slice(columns + h * LANES, columns + (h + 1) * LANES)] = (
                    grad * fg[layer, h, s]
                ).astype(BF16)

        def grad_block(s):
            whole = lax.dot_general(
                lows[rows_of(s), 0:columns],
                vw[layer],
                (((1,), (1,)), ((), ())),
                preferred_element_type=F32,
            ) + lax.dot_general(
                lows[rows_of(s), columns : 2 * columns],
                gw[layer],
                (((1,), (1,)), ((), ())),
                preferred_element_type=F32,
            )
            part[rows_of(s)] = whole.astype(BF16)

        def weights():
            if weights_first:
                for m in range(2):

                    def put_one(i, block):
                        wt[layer, m, i] = block.reshape(wt.shape[3:])

                    weight_term(gath.at[layer], lows[:, m * columns : (m + 1) * columns], put_one)
                    scatters[1 + m].start()
                    if m == 1:
                        scatters[1].after_core()
            else:

                def put(i, block):
                    wt[layer, 0, i] = block[:, 0:columns].reshape(wt.shape[3:])
                    wt[layer, 1, i] = block[:, columns:].reshape(wt.shape[3:])

                weight_term(gath.at[layer], lows[...], put)
                scatters[0].start()

        def block(s):
            if not weights_first:
                lows_block(s)
            grad_block(s)

        if weights_first:
            lax.fori_loop(0, tp, lambda s, carry: lows_block(s) or carry, 0)
        block(far)
        send.send_far()
        if weights_first:
            meanwhile()
            scatters[0].after_core()
            weights()
        block(right)
        block(left)
        send.send_early()
        if weights_first:
            scatters[2].after_core()
        between()
        block(x)
        send.combine_first()
        send.combine_last()
        if not weights_first:
            weights()
        return send, scatters, tap_terms

    tapsum[...] = jnp.zeros(tapsum.shape, F32)
    loads[0].wait()
    fill(frames, hid)
    gather = GatherX(gath, 0)
    for group in (0, 1):
        pair(group, lambda first_row: normalize(0, lambda r: rows_in(hid, r), first_row))
    pl.semaphore_wait(barrier, len(peers))
    for i in (0, 2, 1, 3):
        gather.push(i)
    loads[1].wait()
    fill(og, up)
    gather_up = GatherX(ups, 1)

    def copy_up(first_row):
        ups[1, rows_of(x, first_row, CHUNK)] = rows_in(up, first_row).astype(BF16)

    for group in (0, 1):
        pair(group, copy_up)
    for load in loads[2:]:
        load.wait()

    def send_up():
        for i in (0, 2, 1, 3):
            gather_up.push(i)

    def up_onward():
        for i in (0, 2, 1, 3):
            gather_up.onward(i)

    activate, scale0 = forward(0, gather, send_up, up_onward)
    branch = ScatterX(0)

    def project_block(s):
        activate(s)
        part[rows_of(s)] = jnp.dot(
            act[0, rows_of(s)], pw[0], preferred_element_type=F32
        ).astype(BF16)

    project_block(far)
    branch.send_far()
    project_block(right)
    project_block(left)
    branch.send_early()
    project_block(x)
    branch.combine_first()
    branch.combine_last()

    def hidden(first_row):
        return (rows_in(hid, first_row) + branch.rows(first_row)).astype(BF16).astype(F32)

    gather = GatherX(gath, 1)
    for group in (0, 1):
        branch.landed(group)
        branch.landed(group + 2)
        pair(group, lambda first_row: normalize(1, hidden, first_row))
        gather.push(group)
        gather.push(group + 2)
    branch.sent()

    def nothing():
        return None

    def early_products():
        gather_up.wait_left()
        gather_up.wait_right()
        gather_up.wait_far()
        gather_up.sent()

        def step(s, carry):
            early[rows_of(s)] = act_grad(1, s)
            return carry

        lax.fori_loop(0, tp, step, 0)

    activate, scale1 = forward(1, gather, nothing, early_products)

    def all_blocks(block, carry):
        return lax.fori_loop(0, tp, block, carry)

    send, (scatter1,), tap_terms1 = backward(
        1, 1, all_blocks, scale1, activate, nothing, nothing, False
    )
    gather0 = GatherX(ups, 0)

    def next_up(first_row):
        whole = rows_in(up, first_row) + back_rows(1, send, first_row)
        up[tiles(first_row)] = whole.reshape(CHUNK // 8, 8, depth)
        ups[0, rows_of(x, first_row, CHUNK)] = whole.astype(BF16)

    for group in (0, 1):
        send.landed(group)
        send.landed(group + 2)
        pair(group, next_up)
        gather0.push(group)
        gather0.push(group + 2)
        if group == 0:
            scatter1.after_core()
    taps1 = []

    def in_turn(block, carry):
        gather0.onward(0)
        gather0.onward(2)
        carry = block(x, carry)
        gather0.onward(1)
        gather0.onward(3)
        send.sent()
        taps1.append(tap_terms1())
        gather0.wait_left()
        carry = block(left, carry)
        gather0.wait_right()
        carry = block(right, carry)
        gather0.wait_far()
        carry = block(far, carry)
        gather0.sent()
        return carry

    last, scatters0, tap_terms0 = backward(
        0, 2, in_turn, scale0, None, lambda: taps1[0].middle(), scatter1.after_y, True
    )
    taps0 = tap_terms0()
    scatters0[0].after_y()

    def last_up(first_row):
        whole = rows_in(up, first_row) + back_rows(0, last, first_row)
        up[tiles(first_row)] = whole.reshape(CHUNK // 8, 8, depth)

    scatters0[1].after_y()
    last.landed(0)
    last.landed(2)
    pair(0, last_up)
    taps0.middle()
    scatters0[2].after_z()
    last.landed(1)
    last.landed(3)
    pair(1, last_up)
    last.sent()
    taps1[0].finish()
    scatter1.after_z()
    scatters0[0].after_z()
    scatters0[1].after_z()
    scatters0[2].after_y()
    taps0.finish()


def scratch(ctx, tp, layers, depth, columns):
    ny, nz, nc = grid_of(ctx)
    rows = tp * ROWS
    piece = depth // ctx
    return [
        pltpu.VMEM((layers, depth, columns), BF16),
        pltpu.VMEM((layers, depth, columns), BF16),
        pltpu.VMEM((layers, columns, depth), BF16),
        pltpu.VMEM((STREAMS, SEG, 2, depth), BF16),
        pltpu.VMEM((STREAMS, SEG, 2, depth), BF16),
        pltpu.VMEM((TAPS, layers, columns), F32),
        pltpu.VMEM((layers, columns), F32),
        pltpu.VMEM((layers, columns), F32),
        pltpu.VMEM((SEG, 8, depth), F32),
        pltpu.VMEM((tp + 2, ROWS, LANES), F32),
        pltpu.VMEM((layers, rows, depth), BF16),
        pltpu.VMEM((layers, rows, depth), BF16),
        pltpu.VMEM((rows, depth), BF16),
        pltpu.VMEM((3, ROWS, depth), BF16),
        pltpu.VMEM((3, 2, ROWS, depth), BF16),
        pltpu.VMEM((layers, ROWS, depth), F32),
        pltpu.VMEM((layers, ROWS, LANES), F32),
        pltpu.VMEM((layers, 2, tp, ROWS, LANES), F32),
        pltpu.VMEM((layers, 2, tp, ROWS, LANES), F32),
        pltpu.VMEM((layers, 2, tp, ROWS, LANES), F32),
        pltpu.VMEM((layers, 2, tp, ROWS, LANES), F32),
        pltpu.VMEM((layers, rows, columns), BF16),
        pltpu.VMEM((rows, columns), BF16),
        pltpu.VMEM((3, 2, tp + 2, WIDE, LANES), F32),
        pltpu.VMEM((rows, 2 * columns), BF16),
        pltpu.VMEM((layers, 2, ROWS, columns), BF16),
        pltpu.VMEM((layers, 2, ROWS, 2 * columns), BF16),
        pltpu.VMEM((4, ny * nc, 8, LANES), F32),
        pltpu.VMEM((4, nz, 8, LANES), F32),
        pltpu.VMEM((2, TAPS + 1, LANES), F32),
        pltpu.VMEM((layers, ny * nc, 2, TAPS + 1, LANES), BF16),
        pltpu.VMEM((layers, nz, 2, TAPS + 1, LANES), BF16),
        pltpu.VMEM((layers, 3, ny, nz, nc, piece, columns), BF16),
        pltpu.VMEM((layers, 3, ny, nz, piece, columns), BF16),
        pltpu.VMEM((layers, 3, ny, nz, piece, columns), BF16),
        pltpu.VMEM((layers, ny, 3, nz, piece, columns), BF16),
        pltpu.VMEM((layers, 3, nz, piece, columns), BF16),
        pltpu.VMEM((layers, nz, 3, piece, columns), BF16),
        pltpu.VMEM((rows, columns), F32),
        pltpu.VMEM((nz, ny, piece, columns), BF16),
        pltpu.VMEM((ny, piece, columns), BF16),
        pltpu.VMEM((ny, piece, columns), BF16),
        pltpu.SemaphoreType.DMA((8,)),
        pltpu.SemaphoreType.DMA((256,)),
        pltpu.SemaphoreType.DMA((256,)),
    ]


def flush(*refs):
    count = len(refs) // 2
    for i in range(1, count):
        refs[count + i][...] = refs[i][...]

    def put(t, carry):
        for q in range(STREAMS):
            refs[count][q, t] = refs[0][t, 2 * q : 2 * q + 2, :]
        return carry

    lax.fori_loop(0, SEG, put, 0)


def on_device(
    frames,
    lengths,
    value_weight,
    gate_weight,
    tap_weights,
    norm_gain,
    norm_shift,
    project_weight,
    output_grad,
):
    ctx, tp = lax.axis_size("ctx"), lax.axis_size("tp")
    layers, depth, columns = value_weight.shape
    piece = depth // ctx
    vmem = pl.BlockSpec(memory_space=pltpu.VMEM)
    smem = pl.BlockSpec(memory_space=pltpu.SMEM)
    hbm = pl.BlockSpec(memory_space=pl.ANY)
    recs = frames.shape[1]
    split = (STREAMS, SEG, recs, depth)
    shapes = (
        jax.ShapeDtypeStruct((layers, piece, columns), F32),
        jax.ShapeDtypeStruct((layers, piece, columns), F32),
        jax.ShapeDtypeStruct((layers, piece, columns), F32),
        jax.ShapeDtypeStruct((TAPS, layers, columns), F32),
    )
    results = pl.pallas_call(
        functools.partial(fused, ctx, tp),
        out_shape=(jax.ShapeDtypeStruct((SEG, 8, depth), F32),) + shapes,
        in_specs=[hbm, hbm, smem] + [hbm] * 6,
        out_specs=(vmem,) * 5,
        scratch_shapes=scratch(ctx, tp, layers, depth, columns),
        compiler_params=pltpu.CompilerParams(
            collective_id=0, has_side_effects=True, vmem_limit_bytes=60 * 1024 * 1024
        ),
    )(
        frames.reshape(split),
        output_grad.reshape(split),
        lengths,
        value_weight,
        gate_weight,
        project_weight,
        jnp.swapaxes(tap_weights, 0, 1),
        norm_gain,
        norm_shift,
    )
    up, value, gate, project, tap = pl.pallas_call(
        flush,
        out_shape=(jax.ShapeDtypeStruct(split, F32),) + shapes,
        in_specs=[vmem] * 5,
        out_specs=(vmem,) * 5,
    )(*results)
    return (
        up.reshape(frames.shape),
        value,
        gate,
        jnp.swapaxes(project, 1, 2),
        jnp.swapaxes(tap, 0, 1),
    )


def solution(mesh):
    in_specs = (
        P(("ctx", "tp"), None, None),
        P(),
        P(None, None, "tp"),
        P(None, None, "tp"),
        P(None, None, "tp"),
        P(None, "tp"),
        P(None, "tp"),
        P(None, "tp", None),
        P(("ctx", "tp"), None, None),
    )
    out_specs = (
        P(("ctx", "tp"), None, None),
        P(None, "ctx", "tp"),
        P(None, "ctx", "tp"),
        P(None, "tp", "ctx"),
        P(None, None, "tp"),
    )
    return jax.shard_map(
        on_device, mesh=mesh, in_specs=in_specs, out_specs=out_specs, check_vma=False
    )
```

```python
import functools

import jax
import jax.numpy as jnp
from jax import lax
from jax.experimental import pallas as pl
from jax.experimental.pallas import tpu as pltpu
from jax.sharding import PartitionSpec as P

EPSILON = 1e-05
MESH = pl.DeviceIdType.MESH
F32, BF16 = jnp.float32, jnp.bfloat16
TAPS, REACH = 31, 15
CHUNK = 32
LANES = 128
STREAMS, SEG = 4, 16
ROWS = SEG * 8
MAIN = REACH * 8
WIDE = (SEG + 2 * REACH) * 8


def grid_of(ctx):
    return {64: (4, 8, 2), 8: (2, 2, 2)}[ctx]


def rows_of(slot, first=0, count=ROWS):
    return pl.ds(pl.multiple_of(slot * ROWS + first, 16), count)


def sigmoid(v):
    return 1.0 / (1.0 + jnp.exp(-v))


def fused(
    ctx,
    tp,
    frames_in,
    og_in,
    lengths,
    vw_in,
    gw_in,
    pw_in,
    taps_in,
    gain_in,
    shift_in,
    up,
    value_out,
    gate_out,
    project_out,
    tap_out,
    vw,
    gw,
    pw,
    frames,
    og,
    taps,
    gain,
    shift,
    hid,
    val,
    gath,
    ups,
    part,
    farland,
    land,
    normed,
    lnscale,
    fv,
    fg,
    scaled,
    ds,
    act,
    glu,
    wide,
    lows,
    halo,
    halo2,
    first,
    second,
    tapsum,
    tap1,
    tap2,
    wt,
    in1,
    out2,
    in2,
    out3,
    in3,
    early,
    in2z,
    out3z,
    in3z,
    lsem,
    ssem,
    rsem,
):
    ny, nz, nc = grid_of(ctx)
    pos = lax.axis_index("ctx")
    x = lax.axis_index("tp")
    y, z, c = pos // (nz * nc), (pos // nc) % nz, pos % nc
    depth = gath.shape[2]
    columns = value_out.shape[2]

    def to_x(p):
        return {"tp": p}

    def to_yc(p):
        return {"ctx": ((p // nc) * nz + z) * nc + p % nc}

    def to_y(p):
        return {"ctx": (p * nz + z) * nc + c}

    def to_z(p):
        return {"ctx": (y * nz + p) * nc + c}

    def to_c(p):
        return {"ctx": (y * nz + z) * nc + p}

    yc = y * nc + c
    following = {"ctx": lax.rem(pos + 1, ctx)}
    previous = {"ctx": lax.rem(pos + ctx - 1, ctx)}

    loads = [
        pltpu.make_async_copy(src, dst, lsem.at[i])
        for i, (src, dst) in enumerate(
            (
                (frames_in, frames),
                (og_in, og),
                (vw_in, vw),
                (gw_in, gw),
                (taps_in, taps),
                (gain_in, gain),
                (shift_in, shift),
                (pw_in, pw),
            )
        )
    ]
    for load in loads:
        load.start()

    barrier = pltpu.get_barrier_semaphore()
    peers = [to_x(lax.rem(x + s, tp)) for s in range(1, tp)]
    peers += [to_yc(lax.rem(yc + s, ny * nc)) for s in range(1, ny * nc)]
    peers += [to_z(lax.rem(z + s, nz)) for s in range(1, nz)]
    peers += [following, previous]
    for peer in peers:
        pl.semaphore_signal(barrier, inc=1, device_id=peer, device_id_type=MESH)
    taken = [0]

    def take(n):
        taken[0] += n
        return taken[0] - n

    def remote(src, dst, send, recv, target):
        return pltpu.make_async_remote_copy(
            src_ref=src,
            dst_ref=dst,
            send_sem=ssem.at[send],
            recv_sem=rsem.at[recv],
            device_id=target,
            device_id_type=MESH,
        )

    class Exchange:
        def __init__(self, count, me, target, src, dst):
            self.count, self.me, self.target, self.src, self.dst = count, me, target, src, dst
            self.base = take(count)
            self.order = list(range(1, count))

        def peer(self, step):
            return lax.rem(self.me + step, self.count)

        def send(self, step):
            p = self.peer(step)
            remote(
                self.src(p), self.dst(self.me), self.base + step, self.base + self.me, self.target(p)
            ).start()

        def start(self):
            for step in self.order:
                self.send(step)

        def landed(self, step):
            p = self.peer(step)
            remote(
                self.src(p), self.dst(p), self.base + step, self.base + p, self.target(p)
            ).wait_recv()

        def sent(self):
            for step in self.order:
                p = self.peer(step)
                remote(
                    self.src(p), self.dst(self.me), self.base + step, self.base + self.me, self.target(p)
                ).wait_send()

        def finish(self):
            for step in self.order:
                self.landed(step)
            self.sent()

    right, left, far = lax.rem(x + 1, tp), lax.rem(x + 3, tp), lax.rem(x + 2, tp)

    class GatherX:
        def __init__(self, buf, which):
            self.rows = lambda d, i: buf.at[which, rows_of(d, i * CHUNK, CHUNK)]
            self.base = take(12)

        def copy(self, owner, i, sem, target):
            ref = self.rows(owner, i)
            return remote(ref, ref, self.base + sem, self.base + sem, to_x(target))

        def push(self, i):
            self.copy(x, i, i, right).start()
            self.copy(x, i, 4 + i, left).start()

        def onward(self, i):
            if i < 2:
                self.copy(left, i, i, right).wait_recv()
                self.copy(left, i, 8 + i, right).start()
            else:
                self.copy(right, i, 4 + i, left).wait_recv()
                self.copy(right, i, 8 + i, left).start()

        def wait_left(self):
            for i in (2, 3):
                self.copy(left, i, i, right).wait_recv()

        def wait_right(self):
            for i in (0, 1):
                self.copy(right, i, 4 + i, left).wait_recv()

        def wait_far(self):
            for i in (0, 2, 1, 3):
                self.copy(far, i, 8 + i, right).wait_recv()

        def sent(self):
            for i in range(4):
                self.copy(x, i, i, right).wait_send()
                self.copy(x, i, 4 + i, left).wait_send()
                if i < 2:
                    self.copy(left, i, 8 + i, right).wait_send()
                else:
                    self.copy(right, i, 8 + i, left).wait_send()

    class ScatterX:
        def __init__(self, u):
            self.u = u
            self.base = take(12)

        def far_copy(self, i):
            return remote(
                part.at[rows_of(far, i * CHUNK, CHUNK)],
                farland.at[self.u, pl.ds(i * CHUNK, CHUNK)],
                self.base + i,
                self.base + i,
                to_x(right if i < 2 else left),
            )

        def near_copy(self, way, i):
            sem = self.base + 4 + 4 * way + i
            return remote(
                part.at[rows_of(left if way else right, i * CHUNK, CHUNK)],
                land.at[self.u, way, pl.ds(i * CHUNK, CHUNK)],
                sem,
                sem,
                to_x(left if way else right),
            )

        def send_far(self):
            for i in (0, 2, 1, 3):
                self.far_copy(i).start()

        def send_early(self):
            self.near_copy(0, 2).start()
            self.near_copy(1, 0).start()

        def send_late(self):
            self.near_copy(0, 3).start()
            self.near_copy(1, 1).start()

        def combine(self, i):
            self.far_copy(i).wait_recv()
            way = 0 if i < 2 else 1
            at = rows_of(left if way else right, i * CHUNK, CHUNK)
            part[at] = (
                part[at].astype(F32) + farland[self.u, i * CHUNK : (i + 1) * CHUNK].astype(F32)
            ).astype(BF16)
            self.near_copy(way, i).start()

        def combine_first(self):
            self.combine(0)
            self.combine(2)

        def combine_last(self):
            self.send_late()
            self.combine(1)
            self.combine(3)

        def landed(self, i):
            self.near_copy(0, i).wait_recv()
            self.near_copy(1, i).wait_recv()

        def sent(self):
            for i in range(4):
                self.far_copy(i).wait_send()
                self.near_copy(0, i).wait_send()
                self.near_copy(1, i).wait_send()

        def rows(self, first_row):
            at = pl.ds(pl.multiple_of(first_row, CHUNK), CHUNK)
            return (
                part[rows_of(x, first_row, CHUNK)].astype(F32)
                + land[self.u, 0, at].astype(F32)
                + land[self.u, 1, at].astype(F32)
            )

    len0, len1 = lengths[0], lengths[1]
    start_frame = pos * (tp * STREAMS * SEG)
    t_in = lax.broadcasted_iota(jnp.int32, (SEG, 8, LANES), 0)
    sub = lax.broadcasted_iota(jnp.int32, (SEG, 8, LANES), 1)
    limit = jnp.where(sub % 2 == 0, len0, len1)
    for s in range(-1, tp + 1):
        frame = start_frame + s * (STREAMS * SEG) + (sub // 2) * SEG + t_in
        val[tp + 1 if s == tp else s if s >= 0 else tp] = jnp.where(frame < limit, 1.0, 0.0).astype(F32).reshape(ROWS, LANES)
    span = tp * STREAMS * SEG
    total = (len0 + len1).astype(F32)
    local_count = (
        jnp.clip(len0 - start_frame, 0, span) + jnp.clip(len1 - start_frame, 0, span)
    ).astype(F32)

    def halves(h):
        return slice(h * LANES, (h + 1) * LANES)

    def reduce_tile(u, rows, merge, meanwhile=None, later=None):
        first[u, yc] = jnp.zeros((8, LANES), F32)
        for i, row in enumerate(rows):
            first[u, yc, i : i + 1, :] = row
        one = Exchange(
            ny * nc, yc, to_yc, lambda p: first.at[u, yc], lambda p: first.at[u, p]
        )
        one.start()
        if meanwhile is not None:
            meanwhile()
        one.finish()
        second[u, z] = merge([first[u, i] for i in range(ny * nc)])
        two = Exchange(nz, z, to_z, lambda p: second.at[u, z], lambda p: second.at[u, p])
        two.start()
        if later is not None:
            later()
        two.finish()
        return merge([second[u, i] for i in range(nz)])

    def merge_sum(tiles):
        whole = tiles[0]
        for tile in tiles[1:]:
            whole = whole + tile
        return whole

    def merge_moments(tiles):
        whole = merge_sum(tiles)
        mean = whole[0:2] / jnp.maximum(whole[4:5], 1.0)
        square = whole[2:4]
        for tile in tiles:
            gap = tile[0:2] / jnp.maximum(tile[4:5], 1.0) - mean
            square = square + tile[4:5] * gap * gap
        return jnp.concatenate([whole[0:2], square, whole[4:8]], axis=0)

    def fold(v):
        return jnp.sum(v.reshape(SEG, 8, LANES), axis=0)

    tile_sub = lax.broadcasted_iota(jnp.int32, (REACH, 8, LANES), 1)

    def widen(e, s):
        for h in range(2):
            cur = wide[e, h, s, MAIN + 8 : MAIN + ROWS].reshape(REACH, 8, LANES)
            old = wide[e, h, s - 1, MAIN + 8 : MAIN + ROWS].reshape(REACH, 8, LANES)
            low = jnp.where(tile_sub < 2, pltpu.roll(old, 2, 1), pltpu.roll(cur, 2, 1))
            wide[e, h, s, 0:MAIN] = low.reshape(MAIN, LANES)
            cur = wide[e, h, s, MAIN : MAIN + ROWS - 8].reshape(REACH, 8, LANES)
            new = wide[e, h, s + 1, MAIN : MAIN + ROWS - 8].reshape(REACH, 8, LANES)
            high = jnp.where(tile_sub >= 6, pltpu.roll(new, 6, 1), pltpu.roll(cur, 6, 1))
            wide[e, h, s, MAIN + ROWS : WIDE] = high.reshape(MAIN, LANES)

    def convolve(e, layer, h, s, forward):
        result = None
        for j in range(TAPS):
            at = (j if forward else TAPS - 1 - j) * 8
            term = taps[j, layer : layer + 1, halves(h)] * wide[e, h, s, at : at + ROWS]
            result = term if result is None else result + term
        return result

    class Halo:
        def __init__(self, u, src, dst):
            self.u = u
            base = take(2)
            self.up = remote(src.at[rows_of(tp - 1)], dst.at[u, 0], base, base, following)
            self.down = remote(src.at[rows_of(0)], dst.at[u, 1], base + 1, base + 1, previous)

        def start(self):
            self.up.start()
            self.down.start()

        def wait(self):
            self.up.wait()
            self.down.wait()

    has_low = (pos > 0).astype(F32)
    has_high = (pos < ctx - 1).astype(F32)

    class Scatter:
        def __init__(self, layer, low, high):
            self.layer, self.low, self.high = layer, low, high
            other = lax.rem(c + 1, nc)
            base = take(1)
            mats = slice(low, high)
            self.core = remote(
                wt.at[layer, mats, :, :, other], in1.at[layer, mats], base, base, to_c(other)
            )
            self.ys = Exchange(
                ny, y, to_y, lambda p: out2.at[layer, mats, p], lambda p: in2.at[layer, p, mats]
            )
            self.zs = Exchange(
                nz, z, to_z, lambda p: out3.at[layer, mats, p], lambda p: in3.at[layer, p, mats]
            )

        def start(self):
            self.core.start()

        def after_core(self):
            layer = self.layer
            self.core.wait()

            def add(i, carry):
                a, b = i // ny, i % ny
                out2[layer, a, b] = (
                    wt[layer, a, b, :, c].astype(F32) + in1[layer, a, b].astype(F32)
                ).astype(BF16)
                return carry

            lax.fori_loop(self.low * ny, self.high * ny, add, 0)
            self.ys.start()

        def after_y(self):
            layer = self.layer
            self.ys.finish()

            def add(a, carry):
                whole = out2[layer, a, y].astype(F32)
                for s in range(1, ny):
                    whole = whole + in2[layer, lax.rem(y + s, ny), a].astype(F32)
                out3[layer, a] = whole.astype(BF16)
                return carry

            lax.fori_loop(self.low, self.high, add, 0)
            self.zs.start()

        def after_z(self):
            layer = self.layer
            self.zs.finish()
            outs = (value_out, gate_out, project_out)
            for a, out in list(enumerate(outs))[self.low : self.high]:
                whole = out3[layer, a, z].astype(F32)
                for s in range(1, nz):
                    whole = whole + in3[layer, lax.rem(z + s, nz), a].astype(F32)
                out[layer] = whole

    class CrossScatter:
        def __init__(self, mat):
            self.mat = mat
            other = lax.rem(c + 1, nc)
            base = take(1)
            self.core = remote(
                wt.at[0, mat, :, :, other], in1.at[0, mat], base, base, to_c(other)
            )
            self.zs = Exchange(
                nz, z, to_z, lambda p: out2.at[0, mat, :, p], lambda p: in2z.at[p]
            )
            self.ys = Exchange(ny, y, to_y, lambda p: out3z.at[p], lambda p: in3z.at[p])

        def start(self):
            self.core.start()

        def after_core(self):
            self.core.wait()

            def add(b, carry):
                out2[0, self.mat, b] = (
                    wt[0, self.mat, b, :, c].astype(F32) + in1[0, self.mat, b].astype(F32)
                ).astype(BF16)
                return carry

            lax.fori_loop(0, ny, add, 0)
            self.zs.start()

        def after_z(self):
            self.zs.finish()

            def add(b, carry):
                whole = out2[0, self.mat, b, z].astype(F32)
                for s in range(1, nz):
                    whole = whole + in2z[lax.rem(z + s, nz), b].astype(F32)
                out3z[b] = whole.astype(BF16)
                return carry

            lax.fori_loop(0, ny, add, 0)
            self.ys.start()

        def after_y(self):
            self.ys.finish()
            whole = out3z[y].astype(F32)
            for s in range(1, ny):
                whole = whole + in3z[lax.rem(y + s, ny)].astype(F32)
            gate_out[0] = whole

    def weight_term(left, right, put):
        def step(i, carry):
            cols = pl.ds(pl.multiple_of(i * (depth // ny), depth // ny), depth // ny)
            whole = lax.dot_general(
                left[:, cols], right, (((0,), (0,)), ((), ())), preferred_element_type=F32
            )
            put(i, whole.astype(BF16))
            return carry

        lax.fori_loop(0, ny, step, 0)

    class TapSum:
        def __init__(self, layer):
            self.layer = layer
            self.one = Exchange(
                ny * nc, yc, to_yc, lambda p: tap1.at[layer, yc], lambda p: tap1.at[layer, p]
            )
            self.two = Exchange(
                nz, z, to_z, lambda p: tap2.at[layer, z], lambda p: tap2.at[layer, p]
            )

        def start(self):
            tap1[self.layer, yc] = tapsum[...].astype(BF16)
            self.one.start()

        def middle(self):
            self.one.finish()
            whole = tap1[self.layer, 0].astype(F32)
            for i in range(1, ny * nc):
                whole = whole + tap1[self.layer, i].astype(F32)
            tap2[self.layer, z] = whole.astype(BF16)
            self.two.start()

        def finish(self):
            self.two.finish()
            whole = tap2[self.layer, 0].astype(F32)
            for i in range(1, nz):
                whole = whole + tap2[self.layer, i].astype(F32)
            for h in range(2):
                tap_out[:, self.layer, halves(h)] = whole[h, 0:TAPS]

    def pair(group, step):
        lax.fori_loop(0, 2, lambda k, carry: step((2 * k + group) * CHUNK) or carry, 0)

    def tiles(first_row):
        return pl.ds(first_row // 8, CHUNK // 8)

    def rows_in(ref, first_row):
        return ref[tiles(first_row)].reshape(CHUNK, depth)

    def fill(src, dst):
        def step(t, carry):
            for q in range(STREAMS):
                dst[t, 2 * q : 2 * q + 2, :] = src[q, t].astype(F32)
            return carry

        lax.fori_loop(0, SEG, step, 0)

    def normalize(layer, rows_at, first_row):
        at = pl.ds(pl.multiple_of(first_row, CHUNK), CHUNK)
        rows = rows_at(first_row)
        centered = rows - jnp.mean(rows, axis=1, keepdims=True)
        scale = lax.rsqrt(jnp.mean(centered * centered, axis=1, keepdims=True) + EPSILON)
        out = centered * scale
        normed[layer, at] = out
        lnscale[layer, at] = jnp.broadcast_to(scale, (CHUNK, LANES))
        gath[layer, rows_of(x, first_row, CHUNK)] = out.astype(BF16)

    def back_rows(layer, summed, first_row):
        at = pl.ds(pl.multiple_of(first_row, CHUNK), CHUNK)
        grad = summed.rows(first_row)
        unit = normed[layer, at]
        cross = jnp.mean(grad * unit, axis=1, keepdims=True)
        scale = lnscale[layer, at][:, 0:1]
        return scale * (grad - jnp.mean(grad, axis=1, keepdims=True) - unit * cross)

    def forward(layer, gather, after, later):
        def block(s):
            rows = gath[layer, rows_of(s)]
            value = jnp.dot(rows, vw[layer], preferred_element_type=F32)
            gate = sigmoid(jnp.dot(rows, gw[layer], preferred_element_type=F32))
            for h in range(2):
                v, g = value[:, halves(h)], gate[:, halves(h)]
                keep = g * val[s]
                fv[layer, h, s] = keep
                fg[layer, h, s] = v * (1.0 - g) * keep
                low = (v * keep).astype(BF16)
                glu[rows_of(s), halves(h)] = low
                wide[layer, h, s + 1, MAIN : MAIN + ROWS] = low.astype(F32)

        gather.onward(0)
        gather.onward(2)
        block(x)
        gather.onward(1)
        gather.onward(3)
        gather.wait_left()
        block(left)
        gather.wait_right()
        block(right)
        gather.wait_far()
        block(far)
        edge = Halo(layer, glu, halo)
        edge.start()
        after()

        def conv(s, carry):
            widen(layer, s + 1)
            sums = []
            for h in range(2):
                mixed = convolve(layer, layer, h, s + 1, True)
                scaled[layer, h, s] = mixed
                sums.append(carry[h] + fold(mixed * val[s]))
            return tuple(sums)

        zero = jnp.zeros((8, LANES), F32)
        for h in range(2):
            for side in (0, tp + 1):
                wide[layer, h, side, MAIN : MAIN + ROWS] = jnp.zeros((ROWS, LANES), F32)
        sums = list(lax.fori_loop(0, tp, conv, (zero, zero)))
        edge.wait()
        for h in range(2):
            tap_rows = [taps[j, layer : layer + 1, halves(h)] for j in range(TAPS)]
            low = halo[layer, 0, :, halves(h)].astype(F32) * has_low
            high = halo[layer, 1, :, halves(h)].astype(F32) * has_high
            wide[layer, h, 0, MAIN : MAIN + ROWS] = low
            wide[layer, h, tp + 1, MAIN : MAIN + ROWS] = high
            low = low[8:].reshape(REACH, 8, LANES)
            high = high[: MAIN].reshape(REACH, 8, LANES)
            low = jnp.where(tile_sub < 2, pltpu.roll(low, 2, 1), 0.0)
            high = jnp.where(tile_sub >= 6, pltpu.roll(high, 6, 1), 0.0)
            wide[layer, h, 1, 0:MAIN] += low.reshape(MAIN, LANES)
            wide[layer, h, tp, MAIN + ROWS : WIDE] += high.reshape(MAIN, LANES)
            for t in range(REACH):
                at = slice(t * 8, t * 8 + 8)
                add = None
                for j in range(REACH - t):
                    term = tap_rows[j] * low[t + j]
                    add = term if add is None else add + term
                scaled[layer, h, 0, at] += add
                sums[h] = sums[h] + add * val[0, at]
            for t in range(1, SEG):
                at = slice(t * 8, t * 8 + 8)
                add = None
                for i in range(t):
                    term = tap_rows[SEG + REACH + i - t] * high[i]
                    add = term if add is None else add + term
                scaled[layer, h, tp - 1, at] += add
                sums[h] = sums[h] + add * val[tp - 1, at]
        sums = [jnp.sum(v, axis=0, keepdims=True) for v in sums]
        means = [v / jnp.maximum(local_count, 1.0) for v in sums]

        def spread(s, carry):
            out = []
            for h in range(2):
                gap = (scaled[layer, h, s] - means[h]) * val[s]
                out.append(carry[h] + fold(gap * gap))
            return tuple(out)

        squares = lax.fori_loop(0, tp, spread, (zero, zero))
        squares = [jnp.sum(v, axis=0, keepdims=True) for v in squares]
        count = jnp.zeros((1, LANES), F32) + local_count
        whole = reduce_tile(layer, sums + squares + [count], merge_moments, gather.sent, later)
        mean = [whole[h : h + 1] / total for h in range(2)]
        scale = [lax.rsqrt(whole[2 + h : 3 + h] / total + EPSILON) for h in range(2)]

        def activate(s):
            for h in range(2):
                unit = (scaled[layer, h, s] - mean[h]) * scale[h]
                shifted = gain[layer : layer + 1, halves(h)] * unit + shift[layer : layer + 1, halves(h)]
                sig = sigmoid(shifted)
                keep = sig * val[s]
                scaled[layer, h, s] = unit
                ds[layer, h, s] = keep * (1.0 + shifted * (1.0 - sig))
                act[layer, rows_of(s), halves(h)] = (shifted * keep).astype(BF16)

        return activate, scale

    def act_grad(layer, s):
        return lax.dot_general(
            ups[layer, rows_of(s)], pw[layer], (((1,), (1,)), ((), ())), preferred_element_type=F32
        )

    def backward(layer, u, up_block, chan_scale, activate, meanwhile, between, weights_first):
        zero = jnp.zeros((8, LANES), F32)

        def one_block(s, carry):
            if activate is not None:
                activate(s)
            grad = act_grad(layer, s) if activate is None else early[rows_of(s)]
            sums = list(carry)
            for h in range(2):
                g = grad[:, halves(h)] * ds[layer, h, s]
                unit = scaled[layer, h, s]
                ds[layer, h, s] = g
                lows[rows_of(s), halves(h)] = g.astype(BF16)
                lows[rows_of(s), halves(2 + h)] = unit.astype(BF16)
                sums[h] = sums[h] + fold(g)
                sums[2 + h] = sums[2 + h] + fold(g * unit)
            return tuple(sums)

        sums = up_block(one_block, (zero,) * 4)
        edge = Halo(layer, lows, halo2)
        edge.start()
        sums = [jnp.sum(v, axis=0, keepdims=True) for v in sums]

        if weights_first:
            scatters = [Scatter(layer, 2, 3), Scatter(layer, 0, 1), CrossScatter(1)]
        else:
            scatters = [Scatter(layer, 0, 3)]

        def project():
            def put(i, block):
                wt[layer, 2, i] = block.reshape(wt.shape[3:])

            weight_term(ups.at[layer], act[layer], put)
            if weights_first:
                scatters[0].start()

        whole = reduce_tile(2 + layer, sums, merge_sum, project)
        edge.wait()
        factor = [gain[layer : layer + 1, halves(h)] * chan_scale[h] for h in range(2)]
        first_mean = [whole[h : h + 1] / total for h in range(2)]
        cross_mean = [whole[2 + h : 3 + h] / total for h in range(2)]

        def mixed_grad(h, grad, unit, keep):
            return factor[h] * (grad - first_mean[h] - unit * cross_mean[h]) * keep

        def mix(s, carry):
            for h in range(2):
                wide[2, h, s + 1, MAIN : MAIN + ROWS] = mixed_grad(
                    h, ds[layer, h, s], scaled[layer, h, s], val[s]
                )
            return carry

        lax.fori_loop(0, tp, mix, 0)
        for side, has in enumerate((has_low, has_high)):
            for h in range(2):
                wide[2, h, side * (tp + 1), MAIN : MAIN + ROWS] = mixed_grad(
                    h,
                    halo2[layer, side, :, halves(h)].astype(F32),
                    halo2[layer, side, :, halves(2 + h)].astype(F32),
                    val[tp + side] * has,
                )

        def tap_terms():
            block = 8
            for h in range(2):

                def tap(i, sums):
                    s, t = i // (SEG // block), i % (SEG // block) * block
                    sums = list(sums)
                    grads = [
                        wide[2, h, s + 1, pl.ds(pl.multiple_of(MAIN + (t + k) * 8, 8), 8)]
                        for k in range(block)
                    ]
                    for k in range(block + TAPS - 1):
                        row = wide[layer, h, s + 1, pl.ds(pl.multiple_of((t + k) * 8, 8), 8)]
                        for m in range(block):
                            if 0 <= k - m < TAPS:
                                sums[k - m] = sums[k - m] + row * grads[m]
                    return tuple(sums)

                sums = lax.fori_loop(0, tp * SEG // block, tap, (zero,) * TAPS)
                for j in range(TAPS):
                    tapsum[h, j : j + 1, :] = jnp.sum(sums[j], axis=0, keepdims=True)
            total_taps = TapSum(layer)
            total_taps.start()
            return total_taps

        send = ScatterX(u)

        def lows_block(s):
            widen(2, s + 1)
            for h in range(2):
                grad = convolve(2, layer, h, s + 1, False)
                lows[rows_of(s), halves(h)] = (grad * fv[layer, h, s]).astype(BF16)
                lows[rows_of(s), slice(columns + h * LANES, columns + (h + 1) * LANES)] = (
                    grad * fg[layer, h, s]
                ).astype(BF16)

        def grad_block(s):
            whole = lax.dot_general(
                lows[rows_of(s), 0:columns],
                vw[layer],
                (((1,), (1,)), ((), ())),
                preferred_element_type=F32,
            ) + lax.dot_general(
                lows[rows_of(s), columns : 2 * columns],
                gw[layer],
                (((1,), (1,)), ((), ())),
                preferred_element_type=F32,
            )
            part[rows_of(s)] = whole.astype(BF16)

        def weights():
            if weights_first:
                for m in range(2):

                    def put_one(i, block):
                        wt[layer, m, i] = block.reshape(wt.shape[3:])

                    weight_term(gath.at[layer], lows[:, m * columns : (m + 1) * columns], put_one)
                    scatters[1 + m].start()
                    if m == 1:
                        scatters[1].after_core()
            else:

                def put(i, block):
                    wt[layer, 0, i] = block[:, 0:columns].reshape(wt.shape[3:])
                    wt[layer, 1, i] = block[:, columns:].reshape(wt.shape[3:])

                weight_term(gath.at[layer], lows[...], put)
                scatters[0].start()

        def block(s):
            if not weights_first:
                lows_block(s)
            grad_block(s)

        if weights_first:
            lax.fori_loop(0, tp, lambda s, carry: lows_block(s) or carry, 0)
        block(far)
        send.send_far()
        if weights_first:
            meanwhile()
            scatters[0].after_core()
            weights()
        block(right)
        block(left)
        send.send_early()
        if weights_first:
            scatters[2].after_core()
        between()
        block(x)
        send.combine_first()
        send.combine_last()
        if not weights_first:
            weights()
        return send, scatters, tap_terms

    tapsum[...] = jnp.zeros(tapsum.shape, F32)
    loads[0].wait()
    fill(frames, hid)
    gather = GatherX(gath, 0)
    for group in (0, 1):
        pair(group, lambda first_row: normalize(0, lambda r: rows_in(hid, r), first_row))
    pl.semaphore_wait(barrier, len(peers))
    for i in (0, 2, 1, 3):
        gather.push(i)
    loads[1].wait()
    fill(og, up)
    gather_up = GatherX(ups, 1)

    def copy_up(first_row):
        ups[1, rows_of(x, first_row, CHUNK)] = rows_in(up, first_row).astype(BF16)

    for group in (0, 1):
        pair(group, copy_up)
    for load in loads[2:]:
        load.wait()

    def send_up():
        for i in (0, 2, 1, 3):
            gather_up.push(i)

    def up_onward():
        for i in (0, 2, 1, 3):
            gather_up.onward(i)

    activate, scale0 = forward(0, gather, send_up, up_onward)
    branch = ScatterX(0)

    def project_block(s):
        activate(s)
        part[rows_of(s)] = jnp.dot(
            act[0, rows_of(s)], pw[0], preferred_element_type=F32
        ).astype(BF16)

    project_block(far)
    branch.send_far()
    project_block(right)
    project_block(left)
    branch.send_early()
    project_block(x)
    branch.combine_first()
    branch.combine_last()

    def hidden(first_row):
        return (rows_in(hid, first_row) + branch.rows(first_row)).astype(BF16).astype(F32)

    gather = GatherX(gath, 1)
    for group in (0, 1):
        branch.landed(group)
        branch.landed(group + 2)
        pair(group, lambda first_row: normalize(1, hidden, first_row))
        gather.push(group)
        gather.push(group + 2)
    branch.sent()

    def nothing():
        return None

    def early_products():
        gather_up.wait_left()
        gather_up.wait_right()
        gather_up.wait_far()
        gather_up.sent()

        def step(s, carry):
            early[rows_of(s)] = act_grad(1, s)
            return carry

        lax.fori_loop(0, tp, step, 0)

    activate, scale1 = forward(1, gather, nothing, early_products)

    def all_blocks(block, carry):
        return lax.fori_loop(0, tp, block, carry)

    send, (scatter1,), tap_terms1 = backward(
        1, 1, all_blocks, scale1, activate, nothing, nothing, False
    )
    gather0 = GatherX(ups, 0)

    def next_up(first_row):
        whole = rows_in(up, first_row) + back_rows(1, send, first_row)
        up[tiles(first_row)] = whole.reshape(CHUNK // 8, 8, depth)
        ups[0, rows_of(x, first_row, CHUNK)] = whole.astype(BF16)

    for group in (0, 1):
        send.landed(group)
        send.landed(group + 2)
        pair(group, next_up)
        gather0.push(group)
        gather0.push(group + 2)
        if group == 0:
            scatter1.after_core()
    taps1 = []

    def in_turn(block, carry):
        gather0.onward(0)
        gather0.onward(2)
        carry = block(x, carry)
        gather0.onward(1)
        gather0.onward(3)
        send.sent()
        taps1.append(tap_terms1())
        gather0.wait_left()
        carry = block(left, carry)
        gather0.wait_right()
        carry = block(right, carry)
        gather0.wait_far()
        carry = block(far, carry)
        gather0.sent()
        return carry

    last, scatters0, tap_terms0 = backward(
        0, 2, in_turn, scale0, None, lambda: taps1[0].middle(), scatter1.after_y, True
    )
    taps0 = tap_terms0()
    scatters0[0].after_y()

    def last_up(first_row):
        whole = rows_in(up, first_row) + back_rows(0, last, first_row)
        up[tiles(first_row)] = whole.reshape(CHUNK // 8, 8, depth)

    scatters0[1].after_y()
    last.landed(0)
    last.landed(2)
    pair(0, last_up)
    taps0.middle()
    scatters0[2].after_z()
    last.landed(1)
    last.landed(3)
    pair(1, last_up)
    last.sent()
    taps1[0].finish()
    scatter1.after_z()
    scatters0[0].after_z()
    scatters0[1].after_z()
    scatters0[2].after_y()
    taps0.finish()


def scratch(ctx, tp, layers, depth, columns):
    ny, nz, nc = grid_of(ctx)
    rows = tp * ROWS
    piece = depth // ctx
    return [
        pltpu.VMEM((layers, depth, columns), BF16),
        pltpu.VMEM((layers, depth, columns), BF16),
        pltpu.VMEM((layers, columns, depth), BF16),
        pltpu.VMEM((STREAMS, SEG, 2, depth), BF16),
        pltpu.VMEM((STREAMS, SEG, 2, depth), BF16),
        pltpu.VMEM((TAPS, layers, columns), F32),
        pltpu.VMEM((layers, columns), F32),
        pltpu.VMEM((layers, columns), F32),
        pltpu.VMEM((SEG, 8, depth), F32),
        pltpu.VMEM((tp + 2, ROWS, LANES), F32),
        pltpu.VMEM((layers, rows, depth), BF16),
        pltpu.VMEM((layers, rows, depth), BF16),
        pltpu.VMEM((rows, depth), BF16),
        pltpu.VMEM((3, ROWS, depth), BF16),
        pltpu.VMEM((3, 2, ROWS, depth), BF16),
        pltpu.VMEM((layers, ROWS, depth), F32),
        pltpu.VMEM((layers, ROWS, LANES), F32),
        pltpu.VMEM((layers, 2, tp, ROWS, LANES), F32),
        pltpu.VMEM((layers, 2, tp, ROWS, LANES), F32),
        pltpu.VMEM((layers, 2, tp, ROWS, LANES), F32),
        pltpu.VMEM((layers, 2, tp, ROWS, LANES), F32),
        pltpu.VMEM((layers, rows, columns), BF16),
        pltpu.VMEM((rows, columns), BF16),
        pltpu.VMEM((3, 2, tp + 2, WIDE, LANES), F32),
        pltpu.VMEM((rows, 2 * columns), BF16),
        pltpu.VMEM((layers, 2, ROWS, columns), BF16),
        pltpu.VMEM((layers, 2, ROWS, 2 * columns), BF16),
        pltpu.VMEM((4, ny * nc, 8, LANES), F32),
        pltpu.VMEM((4, nz, 8, LANES), F32),
        pltpu.VMEM((2, TAPS + 1, LANES), F32),
        pltpu.VMEM((layers, ny * nc, 2, TAPS + 1, LANES), BF16),
        pltpu.VMEM((layers, nz, 2, TAPS + 1, LANES), BF16),
        pltpu.VMEM((layers, 3, ny, nz, nc, piece, columns), BF16),
        pltpu.VMEM((layers, 3, ny, nz, piece, columns), BF16),
        pltpu.VMEM((layers, 3, ny, nz, piece, columns), BF16),
        pltpu.VMEM((layers, ny, 3, nz, piece, columns), BF16),
        pltpu.VMEM((layers, 3, nz, piece, columns), BF16),
        pltpu.VMEM((layers, nz, 3, piece, columns), BF16),
        pltpu.VMEM((rows, columns), F32),
        pltpu.VMEM((nz, ny, piece, columns), BF16),
        pltpu.VMEM((ny, piece, columns), BF16),
        pltpu.VMEM((ny, piece, columns), BF16),
        pltpu.SemaphoreType.DMA((8,)),
        pltpu.SemaphoreType.DMA((256,)),
        pltpu.SemaphoreType.DMA((256,)),
    ]


def flush(*refs):
    count = len(refs) // 2
    for i in range(1, count):
        refs[count + i][...] = refs[i][...]

    def put(t, carry):
        for q in range(STREAMS):
            refs[count][q, t] = refs[0][t, 2 * q : 2 * q + 2, :]
        return carry

    lax.fori_loop(0, SEG, put, 0)


def on_device(
    frames,
    lengths,
    value_weight,
    gate_weight,
    tap_weights,
    norm_gain,
    norm_shift,
    project_weight,
    output_grad,
):
    ctx, tp = lax.axis_size("ctx"), lax.axis_size("tp")
    layers, depth, columns = value_weight.shape
    piece = depth // ctx
    vmem = pl.BlockSpec(memory_space=pltpu.VMEM)
    smem = pl.BlockSpec(memory_space=pltpu.SMEM)
    hbm = pl.BlockSpec(memory_space=pl.ANY)
    recs = frames.shape[1]
    split = (STREAMS, SEG, recs, depth)
    shapes = (
        jax.ShapeDtypeStruct((layers, piece, columns), F32),
        jax.ShapeDtypeStruct((layers, piece, columns), F32),
        jax.ShapeDtypeStruct((layers, piece, columns), F32),
        jax.ShapeDtypeStruct((TAPS, layers, columns), F32),
    )
    results = pl.pallas_call(
        functools.partial(fused, ctx, tp),
        out_shape=(jax.ShapeDtypeStruct((SEG, 8, depth), F32),) + shapes,
        in_specs=[hbm, hbm, smem] + [hbm] * 6,
        out_specs=(vmem,) * 5,
        scratch_shapes=scratch(ctx, tp, layers, depth, columns),
        compiler_params=pltpu.CompilerParams(
            collective_id=0, has_side_effects=True, vmem_limit_bytes=60 * 1024 * 1024
        ),
    )(
        frames.reshape(split),
        output_grad.reshape(split),
        lengths,
        value_weight,
        gate_weight,
        project_weight,
        jnp.swapaxes(tap_weights, 0, 1),
        norm_gain,
        norm_shift,
    )
    up, value, gate, project, tap = pl.pallas_call(
        flush,
        out_shape=(jax.ShapeDtypeStruct(split, F32),) + shapes,
        in_specs=[vmem] * 5,
        out_specs=(vmem,) * 5,
    )(*results)
    return (
        up.reshape(frames.shape),
        value,
        gate,
        jnp.swapaxes(project, 1, 2),
        jnp.swapaxes(tap, 0, 1),
    )


def solution(mesh):
    in_specs = (
        P(("ctx", "tp"), None, None),
        P(),
        P(None, None, "tp"),
        P(None, None, "tp"),
        P(None, None, "tp"),
        P(None, "tp"),
        P(None, "tp"),
        P(None, "tp", None),
        P(("ctx", "tp"), None, None),
    )
    out_specs = (
        P(("ctx", "tp"), None, None),
        P(None, "ctx", "tp"),
        P(None, "ctx", "tp"),
        P(None, "tp", "ctx"),
        P(None, None, "tp"),
    )
    return jax.shard_map(
        on_device, mesh=mesh, in_specs=in_specs, out_specs=out_specs, check_vma=False
    )
```
